512 devices in a mesh: dp: 8 (over x, core), expert: 64 (over y, z).
Axes of the slice: x: 4, y: 4, z: 16, core: 2. Of those that a mesh axis runs over, the one named last changes fastest.
Arguments:
- tokens: bfloat16 [8, 8192, 2048], P('dp', 'expert'), may hold values from -6 to 6
- expert_ids: int32 [8, 8192, 8], P('dp', 'expert'), may hold values from 0 to 127, all different within a row; in each aligned block of 128 rows (0 to 127, 128 to 255, ..., all dimensions but the last counted through in order) at most 10 rows name the same one
- route_weights: int32 [8, 8192, 8], P('dp', 'expert'), may hold values from 1 to 8
- gate_weight: bfloat16 [64, 2048, 384], P('expert', 'dp'), may hold values from -0.125 to 0.125
- up_weight: bfloat16 [64, 2048, 384], P('expert', 'dp'), may hold values from -0.125 to 0.125
- cotangent: bfloat16 [8, 64, 640, 384], P('dp', 'expert'), may hold values from -6 to 6
Outputs:
- hidden: bfloat16 [8, 64, 640, 384], P('dp', 'expert')
- token_grads: float32 [8, 8192, 2048], P('dp', 'expert')
- gate_grads: float32 [64, 2048, 384], P('expert', 'dp')
- up_grads: float32 [64, 2048, 384], P('expert', 'dp')
The draws below stay inside these ranges and needn't reach their ends.
Inputs may be any that keep to these rules, and one draw needn't show every extreme that they name: `expert_ids`: each token names 8 different experts; among the 128 tokens of one device no expert is named by more than 10 tokens, a bound that some block reaches.
All inputs are finite; a program needn't handle non-finite values.
Results may differ from the reference program's by a relative error of at most 0.015.
Values may be sent and summed in bfloat16 or wider, within the bound.
No kernel may reach another device: no remote copies, remote signals or barrier semaphores. Data moves between devices by JAX's collectives and lax.ppermute only.
A program may use at most 64 MiB of HBM per device.

```python
import math
import jax
import jax.numpy as jnp
import numpy as np
from jax import lax

D = 2048
H = 384
TOP = 8
TOK_DEV = 128
EXPERTS = 128
WIN_EXPERTS = 64
GROUP_TOK = 8192
C = 10
SLOTS = 640
N_DP = 8
N_EXPERT = 64


def set_ends(result, stream_key, low, top_value):
    index_at = [jax.random.randint(jax.random.fold_in(stream_key, axis), (), 0, length) for axis, length in enumerate(result.shape)]
    main_axis = result.shape.index(max(result.shape))
    beside = index_at[:main_axis] + [(index_at[main_axis] + 1) % result.shape[main_axis]] + index_at[main_axis + 1:]
    return result.at[tuple(index_at)].set(low).at[tuple(beside)].set(top_value)


def steps_of(own_key, shape, pieces, least, largest):
    gain, own = 1.0, jax.random.fold_in(own_key, 6)
    for dim, parts in pieces:
        draws = jnp.exp(jax.random.uniform(jax.random.fold_in(own, dim), (parts,), jnp.float32, least / len(pieces), largest / len(pieces)))
        gain = gain * jnp.repeat(draws, shape[dim] // parts).reshape([-1 if axis == dim else 1 for axis in range(len(shape))])
    return gain


def deal_out(key, own, number, rows, amount, top, reach, lean):
    order = jax.random.permutation(key, amount)
    crowded, ordinary = load_shares(amount, rows * top, reach, lean, True), load_shares(amount, rows * top, reach, lean, False)
    places = jnp.arange(amount)

    def named(sizes, offset_by):
        used = int((sizes > 0).sum())
        fixed = max(1, used // 4)
        shifted = fixed + (places - fixed + offset_by * (used - fixed)) % max(1, amount - fixed)
        return jnp.zeros((amount,), jnp.int32).at[order[jnp.where(places < fixed, places, shifted)]].set(jnp.asarray(sizes, jnp.int32))

    sizes = jnp.where(number % 4 == 0, named(crowded, number // 4), named(ordinary, number - number // 4 - 1))
    mixed = jax.random.permutation(jax.random.fold_in(own, 3), amount)
    source_of, sink = mixed[0:amount // 2 * 2:2], mixed[1:amount // 2 * 2:2]
    margin = jnp.minimum(sizes[source_of] - 1, reach - sizes[sink]) // 2
    margin = jnp.where((source_of == order[0]) | (sink == order[0]) | (sizes[sink] == 0), 0, jnp.maximum(margin, 0))
    shifted = jax.random.randint(jax.random.fold_in(own, 4), (amount // 2,), 0, 1 << 20) % (margin + 1)
    sizes = sizes.at[source_of].add(-shifted).at[sink].add(shifted)
    items = jnp.searchsorted(jnp.cumsum(sizes), jnp.arange(rows * top), side="right").astype(jnp.int32)
    listing = items.reshape(top, rows).T
    listing = listing[jax.random.permutation(jax.random.fold_in(own, 1), rows)]
    offset_by = jax.random.randint(jax.random.fold_in(own, 2), (rows, 1), 0, top)
    return jnp.take_along_axis(listing, (jnp.arange(top)[None, :] + offset_by) % top, axis=1)


def load_shares(number_of, total, most, skew, full):
    portions = [(1 << 20) // math.isqrt(standing ** skew) + 1 for standing in range(1, number_of + 1)]
    largest = most if full else min(most, max(-(-total // number_of), total * portions[0] // sum(portions)))
    least = 1 if total - largest >= number_of - 1 else 0
    counts, rest = [largest] + [least] * (number_of - 1), total - largest - least * (number_of - 1)
    while rest > 0:
        movable = [i for i in range(1, number_of) if counts[i] < largest] or [i for i in range(1, number_of) if counts[i] < most]
        pool, left = sum([portions[i] for i in movable]), rest
        for i in movable:
            addition = min(most - counts[i], max(1, left * portions[i] // pool), rest)
            counts[i] = counts[i] + addition
            rest = rest - addition
    return np.array(counts)


def noise(stream_key, shape, scale, bound, split=(), kind=jnp.bfloat16):
    loudness = steps_of(stream_key, shape, split, -0.22, 0.18) if split else 1.0
    entries = jax.random.normal(stream_key, shape, jnp.float32) * scale * loudness
    return jnp.minimum(jnp.maximum(entries, -bound), bound).astype(kind)


def setup_inputs(seed: int = 0) -> dict:
    key_of = jax.random.split(jax.random.key(seed), 7)
    tokens = noise(key_of[0], (N_DP, GROUP_TOK, D), 1.0, 6.0, ((0, 8), (1, 64)))
    expert_ids_keys = jax.random.split(jax.random.fold_in(key_of[1], 1), N_DP * GROUP_TOK // TOK_DEV)
    expert_ids_turns = jax.random.permutation(jax.random.fold_in(key_of[1], 3), N_DP * GROUP_TOK // TOK_DEV)
    expert_ids = jax.vmap(lambda own, number: deal_out(jax.random.fold_in(key_of[1], 2), own, number, TOK_DEV, EXPERTS, TOP, C, 1))(expert_ids_keys, expert_ids_turns).reshape((N_DP, GROUP_TOK, TOP))
    route_weights = set_ends(jax.random.randint(key_of[2], (N_DP, GROUP_TOK, TOP), 1, 9), jax.random.fold_in(key_of[2], 1), 1, 8).astype(jnp.int32)
    gate_weight = noise(key_of[3], (WIN_EXPERTS, D, H), D ** -0.5, 0.125, ((0, 64), (1, 8)))
    up_weight = noise(key_of[4], (WIN_EXPERTS, D, H), D ** -0.5, 0.125, ((0, 64), (1, 8)))
    cotangent = noise(key_of[5], (N_DP, WIN_EXPERTS, SLOTS, H), 1.0, 6.0, ((0, 8), (1, 64)))
    return {"tokens": tokens, "expert_ids": expert_ids, "route_weights": route_weights, "gate_weight": gate_weight, "up_weight": up_weight, "cotangent": cotangent}


def slot_tables(expert_ids, route_weights):
    blocks = expert_ids.reshape(N_DP, N_EXPERT, TOK_DEV, TOP)
    labels = jnp.arange(EXPERTS, dtype=jnp.int32)
    hit_counts = jnp.sum((blocks[..., None] == labels).astype(jnp.int32), axis=3)
    before = jnp.cumsum(hit_counts, axis=2) - hit_counts
    ranked = jnp.take_along_axis(before, blocks, axis=3)
    block_shape = blocks.shape
    source = jnp.arange(N_EXPERT, dtype=jnp.int32)[None, :, None, None]
    position = jnp.arange(TOK_DEV, dtype=jnp.int32)[None, None, :, None]
    group_idx = jnp.broadcast_to(jnp.arange(N_DP, dtype=jnp.int32)[:, None, None, None], block_shape)
    slot_pos = (source * C + ranked).astype(jnp.int32)
    tok_pos = jnp.broadcast_to(source * TOK_DEV + position, block_shape).astype(jnp.int32)
    table_token = jnp.full((N_DP, WIN_EXPERTS, SLOTS), GROUP_TOK, jnp.int32).at[group_idx, blocks, slot_pos].set(tok_pos, mode='drop')
    route_scale = route_weights.reshape(block_shape).astype(jnp.float32) / 8.0
    table_weight = jnp.zeros((N_DP, WIN_EXPERTS, SLOTS), jnp.float32).at[group_idx, blocks, slot_pos].set(route_scale, mode='drop')
    return table_token, table_weight


def reference(tokens, expert_ids, route_weights, gate_weight, up_weight, cotangent):
    table_token, table_weight = slot_tables(expert_ids, route_weights)
    padded = jnp.concatenate([tokens, jnp.zeros((N_DP, 1, D), tokens.dtype)], axis=1)
    pick_rows = jax.vmap(lambda table_rows, row_index: table_rows[row_index])
    add_rows = jax.vmap(lambda running, row_index, values: running.at[row_index].add(values))

    def expert_step(running, inputs):
        row_index, weight, gate_w, up_w, cot_slots = inputs
        slot_rows = pick_rows(padded, row_index).astype(jnp.float32)
        weight_col = weight[..., None]
        gate_pre = jnp.einsum('gsd,dh->gsh', slot_rows, gate_w.astype(jnp.float32))
        up_pre = jnp.einsum('gsd,dh->gsh', slot_rows, up_w.astype(jnp.float32))
        hidden = (jax.nn.silu(gate_pre) * up_pre * weight_col).astype(jnp.bfloat16)
        sigmoid_gate = jax.nn.sigmoid(gate_pre)
        activation = gate_pre * sigmoid_gate
        act_slope = sigmoid_gate * (1.0 + gate_pre * (1.0 - sigmoid_gate))
        scaled = cot_slots.astype(jnp.float32) * weight_col
        grad_gate = (scaled * up_pre * act_slope).astype(jnp.bfloat16)
        grad_up = (scaled * activation).astype(jnp.bfloat16)
        slot_grads = jnp.einsum('gsh,dh->gsd', grad_gate.astype(jnp.float32), gate_w.astype(jnp.float32))
        slot_grads = slot_grads + jnp.einsum('gsh,dh->gsd', grad_up.astype(jnp.float32), up_w.astype(jnp.float32))
        slot_grads = slot_grads.astype(jnp.bfloat16)
        running = add_rows(running, row_index, slot_grads.astype(jnp.float32))
        gate_terms = lax.optimization_barrier(jnp.einsum('gsd,gsh->gdh', slot_rows, grad_gate.astype(jnp.float32)).astype(jnp.bfloat16))
        up_terms = lax.optimization_barrier(jnp.einsum('gsd,gsh->gdh', slot_rows, grad_up.astype(jnp.float32)).astype(jnp.bfloat16))
        gate_sum = jnp.sum(gate_terms.astype(jnp.float32), axis=0)
        up_sum = jnp.sum(up_terms.astype(jnp.float32), axis=0)
        return running, (hidden, gate_sum, up_sum)

    start_grads = jnp.zeros((N_DP, GROUP_TOK + 1, D), jnp.float32)
    inputs = (jnp.transpose(table_token, (1, 0, 2)), jnp.transpose(table_weight, (1, 0, 2)), gate_weight, up_weight, jnp.transpose(cotangent, (1, 0, 2, 3)))
    running, outputs = lax.scan(expert_step, start_grads, inputs)
    hidden_all, gate_grads, up_grads = outputs
    hidden = jnp.transpose(hidden_all, (1, 0, 2, 3))
    token_grads = running[:, :GROUP_TOK]
    return hidden, token_grads, gate_grads, up_grads
```

```python
import functools

import jax
import jax.numpy as jnp
from jax import lax
from jax.experimental import pallas as pl
from jax.experimental.pallas import tpu as pltpu
from jax.sharding import Mesh, PartitionSpec as P

N_Y = 4
N_Z = 16
FORWARD_SPLIT = (1024, 1024)
BACKWARD_SPLIT = (1024, 1024)
VMEM_BYTES = 48 * 1024 * 1024


def starts_of(widths):
    return [sum(widths[:i]) for i in range(len(widths))]


def routing_kernel(ids_ref, weights_ref, out_ref):
    rows, tokens = out_ref.shape
    row = lax.broadcasted_iota(jnp.int32, (rows, tokens), 0)
    kind = row % 8
    device = row // 8
    expert = jnp.where(kind < N_Y, kind * N_Z + device % N_Z, device)
    hits = jnp.zeros((rows, tokens), jnp.float32)
    eighths = jnp.zeros((rows, tokens), jnp.float32)
    for choice in range(ids_ref.shape[0]):
        named = ids_ref[choice : choice + 1, :] == expert
        hits = hits + jnp.where(named, 1.0, 0.0)
        eighths = eighths + jnp.where(named, weights_ref[choice : choice + 1, :].astype(jnp.float32), 0.0)
    earlier = lax.broadcasted_iota(jnp.int32, (tokens, tokens), 0)
    later = lax.broadcasted_iota(jnp.int32, (tokens, tokens), 1)
    triangle = jnp.where(earlier < later, 1.0, 0.0).astype(jnp.bfloat16)
    rank = jnp.dot(hits.astype(jnp.bfloat16), triangle, preferred_element_type=jnp.float32)
    rank = jnp.where(hits > 0.0, rank, -1.0)
    out_ref[...] = jnp.where(kind <= N_Y, rank, eighths).astype(jnp.bfloat16)


def slot_matrix(slot_ref, part, part_slots, part_tokens):
    columns = slice(part * part_tokens, (part + 1) * part_tokens)
    slot = lax.broadcasted_iota(jnp.int32, (part_slots, part_tokens), 0) + part * part_slots
    return jnp.concatenate(
        [jnp.where(slot_ref[y : y + 1, columns] == slot, 1.0, 0.0).astype(jnp.bfloat16) for y in range(N_Y)],
        axis=0,
    )


def pick_kernel(parts, slot_ref, tokens_ref, out_ref):
    part_slots = out_ref.shape[1] // parts
    part_tokens = tokens_ref.shape[0] // parts
    for part in range(parts):
        select = slot_matrix(slot_ref, part, part_slots, part_tokens)
        picked = jnp.dot(
            select,
            tokens_ref[part * part_tokens : (part + 1) * part_tokens, :],
            preferred_element_type=jnp.float32,
        ).astype(jnp.bfloat16)
        for y in range(N_Y):
            out_ref[y, part * part_slots : (part + 1) * part_slots, :] = picked[
                y * part_slots : (y + 1) * part_slots, :
            ]


def add_kernel(parts, slot_ref, grads_ref, out_ref):
    part_slots = grads_ref.shape[1] // parts
    part_tokens = out_ref.shape[0] // parts
    for part in range(parts):
        select = slot_matrix(slot_ref, part, part_slots, part_tokens)
        rows = jnp.concatenate(
            [grads_ref[y, part * part_slots : (part + 1) * part_slots, :] for y in range(N_Y)], axis=0
        )
        out_ref[part * part_tokens : (part + 1) * part_tokens, :] = lax.dot_general(
            select, rows, (((0,), (0,)), ((), ())), preferred_element_type=jnp.float32
        ).astype(jnp.bfloat16)


def call(kernel, out_shape, *operands):
    whole = pl.BlockSpec(memory_space=pltpu.VMEM)
    return pl.pallas_call(
        kernel,
        out_shape=out_shape,
        in_specs=[whole] * len(operands),
        out_specs=whole,
        compiler_params=pltpu.CompilerParams(vmem_limit_bytes=VMEM_BYTES),
    )(*operands)


def shards(tokens, expert_ids, route_weights, gate_weight, up_weight, cotangent):
    experts = N_Y * N_Z
    groups = lax.axis_size("dp")
    slot_count = cotangent.shape[2]
    capacity = slot_count // experts
    row_slots = N_Z * capacity
    block, model_width = tokens.shape[1], tokens.shape[2]
    hidden_units = gate_weight.shape[2]

    gathered = [
        lax.all_gather(tokens[0, :, start : start + width], "z", axis=0, tiled=True)
        for start, width in zip(starts_of(FORWARD_SPLIT), FORWARD_SPLIT)
    ]

    told = call(
        routing_kernel,
        jax.ShapeDtypeStruct((experts * 8, block), jnp.bfloat16),
        expert_ids[0].T,
        route_weights[0].T,
    )
    heard = lax.all_to_all(told.reshape(experts, 8, block), ("y", "z"), 0, 0, tiled=True)
    own_row = lax.dynamic_slice_in_dim(heard, lax.axis_index("y") * N_Z, N_Z, axis=0)
    rank = jnp.transpose(own_row[:, :N_Y], (1, 0, 2)).astype(jnp.int32)
    base = capacity * jnp.arange(N_Z, dtype=jnp.int32)[None, :, None]
    slot_of = jnp.where(rank >= 0, rank + base, -1).reshape(N_Y, N_Z * block)
    places = jnp.arange(capacity, dtype=jnp.int32).astype(jnp.bfloat16)
    weight_col = jnp.sum(
        jnp.where(heard[:, N_Y, None, :] == places[None, :, None], heard[:, N_Y + 1, None, :].astype(jnp.float32), 0.0),
        axis=2,
    ).reshape(slot_count, 1) / 8.0

    stacked = jnp.concatenate((gate_weight[0], up_weight[0]), axis=1)
    full_weights = lax.all_to_all(
        jnp.broadcast_to(stacked[None], (groups,) + stacked.shape), "dp", 0, 0, tiled=True
    ).reshape(model_width, 2 * hidden_units)

    pre = jnp.zeros((slot_count, 2 * hidden_units), jnp.float32)
    slot_rows = []
    for start, width, part in zip(starts_of(FORWARD_SPLIT), FORWARD_SPLIT, gathered):
        picked = call(
            functools.partial(pick_kernel, 2),
            jax.ShapeDtypeStruct((N_Y, row_slots, width), jnp.bfloat16),
            slot_of,
            part,
        )
        rows = lax.all_to_all(picked, "y", 0, 0, tiled=True).reshape(slot_count, width)
        slot_rows.append(rows)
        pre = pre + jnp.dot(rows, full_weights[start : start + width], preferred_element_type=jnp.float32)

    gate_pre, up_pre = pre[:, :hidden_units], pre[:, hidden_units:]
    sigmoid_gate = jax.nn.sigmoid(gate_pre)
    activation = gate_pre * sigmoid_gate
    hidden = (activation * up_pre * weight_col).astype(jnp.bfloat16)
    act_slope = sigmoid_gate * (1.0 + gate_pre * (1.0 - sigmoid_gate))
    scaled = cotangent[0, 0].astype(jnp.float32) * weight_col
    grad_gate = (scaled * up_pre * act_slope).astype(jnp.bfloat16)
    grad_up = (scaled * activation).astype(jnp.bfloat16)
    grad_pre = jnp.concatenate((grad_gate, grad_up), axis=1)

    token_grads = []
    for start, width in zip(starts_of(BACKWARD_SPLIT), BACKWARD_SPLIT):
        grad_rows = lax.dot_general(
            grad_pre,
            full_weights[start : start + width],
            (((1,), (1,)), ((), ())),
            preferred_element_type=jnp.float32,
        ).astype(jnp.bfloat16)
        returned = lax.all_to_all(grad_rows.reshape(N_Y, row_slots, width), "y", 0, 0, tiled=True)
        sums = call(
            functools.partial(add_kernel, 2),
            jax.ShapeDtypeStruct((N_Z * block, width), jnp.bfloat16),
            slot_of,
            returned,
        )
        token_grads.append(lax.psum_scatter(sums, "z", scatter_dimension=0, tiled=True).astype(jnp.float32))

    terms = [
        lax.dot_general(rows, grad_pre, (((0,), (0,)), ((), ())), preferred_element_type=jnp.float32).astype(
            jnp.bfloat16
        )
        for rows in slot_rows
    ]
    terms = jnp.concatenate(terms, axis=0).reshape(groups, model_width // groups, 2 * hidden_units)
    weight_grads = jnp.sum(lax.all_to_all(terms, "dp", 0, 0, tiled=True).astype(jnp.float32), axis=0)
    return (
        hidden[None, None],
        jnp.concatenate(token_grads, axis=1)[None],
        weight_grads[None, :, :hidden_units],
        weight_grads[None, :, hidden_units:],
    )


def solution(mesh):
    grid = Mesh(mesh.devices.reshape(mesh.shape["dp"], N_Y, N_Z), ("dp", "y", "z"))
    expert = ("y", "z")
    in_specs = (
        P("dp", expert, None),
        P("dp", expert, None),
        P("dp", expert, None),
        P(expert, "dp", None),
        P(expert, "dp", None),
        P("dp", expert, None, None),
    )
    out_specs = (
        P("dp", expert, None, None),
        P("dp", expert, None),
        P(expert, "dp", None),
        P(expert, "dp", None),
    )
    return jax.shard_map(shards, mesh=grid, in_specs=in_specs, out_specs=out_specs, check_vma=False)
```

```python
import functools

import jax
import jax.numpy as jnp
import numpy as np
from jax import lax
from jax.experimental import pallas as pl
from jax.experimental.pallas import tpu as pltpu
from jax.sharding import Mesh, PartitionSpec as P

N_Y = 4
N_Z = 16
SLOTS = 10
REACH = 5
NEAR = (0, 1, -1, 2, -2, 3, -3, 4, -4, 5, -5)
FAR = (6, 7, 8, -7, -6)
NEAR_ROWS = 112
FAR_ROWS = 56
MESSAGE = (112, 64, 32)
VMEM_BYTES = 48 * 1024 * 1024
F32 = jnp.float32
BF16 = jnp.bfloat16


def call(kernel, out_shape, *operands, scalars=0, scratch=()):
    whole = pl.BlockSpec(memory_space=pltpu.VMEM)
    small = pl.BlockSpec(memory_space=pltpu.SMEM)
    return pl.pallas_call(
        kernel,
        out_shape=out_shape,
        in_specs=[small] * scalars + [whole] * (len(operands) - scalars),
        out_specs=jax.tree.map(lambda _: whole, out_shape),
        scratch_shapes=list(scratch),
        compiler_params=pltpu.CompilerParams(vmem_limit_bytes=VMEM_BYTES),
    )(*operands)


def array(shape, dtype=BF16):
    return jax.ShapeDtypeStruct(shape, dtype)


def iota(shape, dimension):
    return lax.broadcasted_iota(jnp.int32, shape, dimension)


def one_hot(condition):
    return jnp.where(condition, 1.0, 0.0).astype(BF16)


def dot(a, b, contract=(1, 0)):
    return lax.dot_general(a, b, (((contract[0],), (contract[1],)), ((), ())), preferred_element_type=F32)


def earlier_tokens(tokens):
    return one_hot(iota((tokens, tokens), 0) < iota((tokens, tokens), 1))


def routing_kernel(place_ref, heard_ref, source_ref, slot_ref, near_ref, far_ref, weight_ref, hits_ref):
    y, z = place_ref[0], place_ref[1]
    tokens = heard_ref.shape[2]
    top = heard_ref.shape[1] // 2
    triangle = earlier_tokens(tokens)

    hits_ref[...] = jnp.zeros_like(hits_ref)

    def look(row, offset, expert):
        ids = heard_ref[y * N_Z + lax.rem(z + offset + N_Z, N_Z)][:top].astype(jnp.int32)
        hits_ref[row : row + 1, :] = jnp.sum(jnp.where(ids == expert, 1.0, 0.0), axis=0, keepdims=True)

    for index, offset in enumerate(NEAR):
        for other in range(N_Y):
            look(8 * index + other, offset, other * N_Z + z)
    near_count = 8 * len(NEAR)
    for way, sign in enumerate((1, -1)):
        for place in range(SLOTS):
            step, other = place // N_Y, place % N_Y
            if step == 2 and sign < 0:
                other = other + 2
            expert = other * N_Z + lax.rem(z + sign * (step + 1) + N_Z, N_Z)
            look(near_count + 16 * way + place, -sign * REACH, expert)
    hits = hits_ref[...]
    rank = dot(hits.astype(BF16), triangle).astype(jnp.int32)
    row = iota((near_count, tokens), 0)
    base = (row & 7) * NEAR_ROWS + (row >> 3) * SLOTS
    near_ref[...] = jnp.where(hits[:near_count] > 0.0, base + rank[:near_count], -1)
    row = iota((32, tokens), 0) & 15
    far_ref[...] = jnp.where(hits[near_count:] > 0.0, row * SLOTS + rank[near_count:], -1)

    own = y * N_Z + z
    heard = heard_ref[...].astype(F32)
    named = heard[:, :top] == own.astype(F32)
    own_hits = jnp.sum(jnp.where(named, 1.0, 0.0), axis=1)
    own_weight = jnp.sum(jnp.where(named, heard[:, top:], 0.0), axis=1)
    own_rank = dot(own_hits.astype(BF16), triangle)
    rows = source_ref.shape[0]
    spread = one_hot(iota((rows, own_hits.shape[0]), 1) == source_ref[...])
    rank_of = dot(spread, own_rank.astype(BF16))
    weight_of = dot(spread, own_weight.astype(BF16))
    weight = jnp.where(rank_of == slot_ref[...].astype(F32), weight_of, 0.0)
    weight_ref[...] = jnp.sum(weight, axis=1, keepdims=True) * 0.125


def marked(position_ref, first, count, rows):
    row = iota((rows, position_ref.shape[1]), 0)
    mark = position_ref[first : first + 1, :] == row
    for index in range(1, count):
        mark = mark | (position_ref[first + index : first + index + 1, :] == row)
    return one_hot(mark)


def relative_kernel(row_ref, values_ref, out_ref):
    move = one_hot(iota((row_ref.shape[0], values_ref.shape[0]), 1) == row_ref[...])
    out_ref[...] = dot(move, values_ref[...]).astype(BF16)


def absolute_kernel(row_ref, near_ref, far_ref, out_ref):
    move = one_hot(iota((row_ref.shape[0], out_ref.shape[0]), 1) == row_ref[...])
    count = near_ref.shape[0]
    out = dot(move[:count], near_ref[...], (0, 0)) + dot(move[count:], far_ref[...], (0, 0))
    out_ref[...] = out.astype(BF16)


def far_message_kernel(way, far_ref, tokens_ref, out_ref):
    out_ref[...] = dot(marked(far_ref, 16 * way, SLOTS, out_ref.shape[0]), tokens_ref[...]).astype(BF16)


def near_pick_kernel(near_ref, *refs):
    out_ref = refs[-1]
    select = jnp.concatenate([marked(near_ref, 8 * i, N_Y, out_ref.shape[0]) for i in range(len(NEAR))], axis=1)
    tokens = jnp.concatenate([ref[...] for ref in refs[:-1]], axis=0)
    out_ref[...] = dot(select, tokens).astype(BF16)


def far_places():
    places = {}
    for hop in range(3):
        for way in range(2):
            source = FAR.index((REACH + 1 + hop) * (-1 if way == 0 else 1) if hop < 2 else 8)
            place = np.full((N_Y * FAR_ROWS, 1), -1, np.int32)
            for y in range(N_Y):
                if hop == 2 and y // 2 != way:
                    continue
                for slot in range(SLOTS):
                    row = y * SLOTS + slot if hop < 2 else 8 + (y % 2) * SLOTS + slot
                    place[y * FAR_ROWS + source * SLOTS + slot, 0] = row
            places[hop, way] = place
    return places


FAR_KEYS = tuple((hop, way) for hop in range(3) for way in range(2))


def far_pick_kernel(place_ref, *refs):
    out_ref = refs[-1]
    total = None
    for index, ref in enumerate(refs[:-1]):
        move = one_hot(iota((out_ref.shape[0], ref.shape[0]), 1) == place_ref[:, index : index + 1])
        part = dot(move, ref[...])
        total = part if total is None else total + part
    out_ref[...] = total.astype(BF16)


def far_part_kernel(place_ref, grads_ref, *out_refs):
    for index, ref in enumerate(out_refs):
        move = one_hot(iota((grads_ref.shape[0], ref.shape[0]), 1) == place_ref[:, index : index + 1])
        ref[...] = dot(move, grads_ref[...], (0, 0)).astype(BF16)


def expert_kernel(rows_ref, matrix_ref, weight_ref, cotangent_ref, hidden_ref, grad_ref, row_grads_ref):
    units = hidden_ref.shape[1]
    pre = dot(rows_ref[...], matrix_ref[...])
    gate_pre, up_pre = pre[:, :units], pre[:, units:]
    weight = weight_ref[...]
    sigmoid_gate = jax.nn.sigmoid(gate_pre)
    activation = gate_pre * sigmoid_gate
    hidden_ref[...] = (activation * up_pre * weight).astype(BF16)
    act_slope = sigmoid_gate * (1.0 + gate_pre * (1.0 - sigmoid_gate))
    scaled = cotangent_ref[...].astype(F32) * weight
    grad_ref[:, :units] = (scaled * up_pre * act_slope).astype(BF16)
    grad_ref[:, units:] = (scaled * activation).astype(BF16)
    row_grads_ref[...] = dot(grad_ref[...], matrix_ref[...], (1, 1)).astype(BF16)


def near_sum(index, near_ref, grads_ref):
    return dot(marked(near_ref, 8 * index, N_Y, grads_ref.shape[0]), grads_ref[...], (0, 0))


def first_sum_kernel(index, way, near_ref, far_ref, grads_ref, message_ref, out_ref):
    far = dot(marked(far_ref, 16 * way, SLOTS, message_ref.shape[0]), message_ref[...], (0, 0))
    out_ref[...] = (far + near_sum(index, near_ref, grads_ref)).astype(BF16)


def next_sum_kernel(index, near_ref, grads_ref, sum_ref, out_ref):
    out_ref[...] = (sum_ref[...].astype(F32) + near_sum(index, near_ref, grads_ref)).astype(BF16)


def last_sum_kernel(near_ref, grads_ref, up_ref, down_ref, out_ref):
    out_ref[...] = up_ref[...].astype(F32) + down_ref[...].astype(F32) + near_sum(0, near_ref, grads_ref)


def after(value, *others):
    return lax.optimization_barrier((value,) + others)[0]


def shards(tokens, expert_ids, route_weights, gate_weight, up_weight, cotangent):
    slot_count, units = cotangent.shape[2:]
    block, model_width = tokens.shape[1:]
    near_count, far_count = N_Y * NEAR_ROWS, N_Y * FAR_ROWS
    y, z = lax.axis_index("y"), lax.axis_index("z")

    def send(value, sign):
        return lax.ppermute(value, "z", [(i, (i + sign) % N_Z) for i in range(N_Z)])

    told = jnp.concatenate((expert_ids[0].T, route_weights[0].T), axis=0).astype(BF16)
    heard = lax.all_gather(told, ("y", "z"), axis=0)
    stacked = jnp.concatenate((gate_weight[0], up_weight[0]), axis=1)
    matrix = lax.all_gather(stacked, "dp", axis=0, tiled=True)

    group, offset, slot = np.full((3, near_count + far_count), -1, np.int32)
    for first, rows, sources in ((0, NEAR_ROWS, NEAR), (near_count, FAR_ROWS, FAR)):
        for other in range(N_Y):
            for index, source in enumerate(sources):
                at = first + other * rows + index * SLOTS
                group[at : at + SLOTS], offset[at : at + SLOTS] = other, source
                slot[at : at + SLOTS] = np.arange(SLOTS)
    source_of = jnp.where(group >= 0, group * N_Z + (z + offset + N_Z) % N_Z, -1).astype(jnp.int32)
    row_of = jnp.where(group >= 0, source_of * SLOTS + slot, -1).astype(jnp.int32)[:, None]
    near, far, weight = call(
        routing_kernel,
        (
            array((8 * len(NEAR), block), jnp.int32),
            array((32, block), jnp.int32),
            array((near_count + far_count, 1), F32),
        ),
        jnp.stack((y, z)).astype(jnp.int32),
        heard,
        source_of[:, None],
        jnp.asarray(slot)[:, None],
        scalars=1,
        scratch=(pltpu.VMEM((8 * len(NEAR) + 32, block), F32),),
    )
    cotangent_rows = call(
        relative_kernel, array((near_count + far_count, units)), row_of, cotangent[0, 0]
    )

    blocks = {0: tokens[0]}
    going = [tokens[0], tokens[0]]
    for hop in range(1, REACH + 1):
        going = [send(going[0], 1), send(going[1], -1)]
        blocks[-hop], blocks[hop] = going
    arrived = []
    going = [
        call(functools.partial(far_message_kernel, way), array((MESSAGE[0], model_width)), far, going[way])
        for way in range(2)
    ]
    for hop in range(3):
        going = [send(going[0], 1), send(going[1], -1)]
        arrived += going
        if hop == 0:
            going = [part[40:104] for part in going]
        elif hop == 1:
            going = [part[32:] for part in going]

    def exchange(rows):
        parts = rows.reshape(N_Y, rows.shape[0] // N_Y, model_width)
        return lax.all_to_all(parts, "y", 0, 0, tiled=True).reshape(rows.shape)

    near_rows = exchange(
        call(near_pick_kernel, array((near_count, model_width)), near, *[blocks[source] for source in NEAR])
    )
    places = far_places()
    place_of = jnp.asarray(np.concatenate([places[key] for key in FAR_KEYS], axis=1))
    far_rows = exchange(call(far_pick_kernel, array((far_count, model_width)), place_of, *arrived))

    def expert(rows, first):
        count = rows.shape[0]
        part = slice(first, first + count)
        return call(
            expert_kernel,
            (array((count, units)), array((count, 2 * units)), array((count, model_width))),
            rows,
            matrix,
            weight[part],
            cotangent_rows[part],
        )

    near_hidden, near_grads, near_back = expert(near_rows, 0)
    far_hidden, far_grads, far_back = expert(far_rows, near_count)

    far_back = exchange(far_back)
    near_back = exchange(after(near_back, far_back))
    parts = call(
        far_part_kernel,
        tuple(array((48 if hop < 2 else MESSAGE[2], model_width)) for hop, _ in FAR_KEYS),
        place_of,
        far_back,
    )
    going = list(parts[4:])
    for hop in (2, 1, 0):
        going = [send(going[0], -1), send(going[1], 1)]
        if hop == 2:
            going = [jnp.concatenate((parts[2 + way][:40], going[way][8:]), axis=0) for way in range(2)]
        elif hop == 1:
            blank = jnp.zeros((8, model_width), BF16)
            going = [jnp.concatenate((parts[way][:40], going[way], blank), axis=0) for way in range(2)]
    going = [
        call(
            functools.partial(first_sum_kernel, NEAR.index(REACH * (-1 if way == 0 else 1)), way),
            array((block, model_width)),
            near,
            far,
            near_back,
            going[way],
        )
        for way in range(2)
    ]
    for hop in range(REACH - 1, -1, -1):
        going = [send(going[0], -1), send(going[1], 1)]
        if hop:
            going = [
                call(
                    functools.partial(next_sum_kernel, NEAR.index(hop * (-1 if way == 0 else 1))),
                    array((block, model_width)),
                    near,
                    near_back,
                    going[way],
                )
                for way in range(2)
            ]
    token_grads = call(last_sum_kernel, array((block, model_width), F32), near, near_back, *going)

    far_rows, near_rows = after(far_rows, far_back), after(near_rows, far_back)
    terms = (dot(near_rows, near_grads, (0, 0)) + dot(far_rows, far_grads, (0, 0))).astype(BF16)
    weight_grads = lax.psum_scatter(terms, "dp", scatter_dimension=0, tiled=True).astype(F32)
    hidden = call(
        absolute_kernel,
        array((slot_count, units)),
        row_of,
        after(near_hidden, far_back),
        far_hidden,
    )
    return (
        hidden[None, None],
        token_grads[None],
        weight_grads[None, :, :units],
        weight_grads[None, :, units:],
    )


def solution(mesh):
    grid = Mesh(mesh.devices.reshape(mesh.shape["dp"], N_Y, N_Z), ("dp", "y", "z"))
    expert = ("y", "z")
    in_specs = (
        P("dp", expert, None),
        P("dp", expert, None),
        P("dp", expert, None),
        P(expert, "dp", None),
        P(expert, "dp", None),
        P("dp", expert, None, None),
    )
    out_specs = (
        P("dp", expert, None, None),
        P("dp", expert, None),
        P(expert, "dp", None),
        P(expert, "dp", None),
    )
    return jax.shard_map(shards, mesh=grid, in_specs=in_specs, out_specs=out_specs, check_vma=False)
```

```python
import functools

import jax
import jax.numpy as jnp
import numpy as np
from jax import lax
from jax.experimental import pallas as pl
from jax.experimental.pallas import tpu as pltpu
from jax.sharding import Mesh, PartitionSpec as P

N_Y = 4
N_Z = 16
SLOTS = 10
REACH = 5
NEAR = (0, 1, -1, 2, -2, 3, -3, 4, -4)
LAST = (5, -5, 6, 7, 8, -7, -6)
NEAR_ROWS = 96
LAST_ROWS = 72
MESSAGE = (48, 48, 32)
MESSAGE_SLOTS = (40, 40, 20)
MESSAGE_ROWS = sum(MESSAGE)
LANES = 128
VMEM_BYTES = 48 * 1024 * 1024
F32 = jnp.float32
BF16 = jnp.bfloat16


def call(kernel, out_shape, *operands, scalars=0):
    whole = pl.BlockSpec(memory_space=pltpu.VMEM)
    small = pl.BlockSpec(memory_space=pltpu.SMEM)
    return pl.pallas_call(
        kernel,
        out_shape=out_shape,
        in_specs=[small] * scalars + [whole] * (len(operands) - scalars),
        out_specs=jax.tree.map(lambda _: whole, out_shape),
        compiler_params=pltpu.CompilerParams(vmem_limit_bytes=VMEM_BYTES),
    )(*operands)


def array(shape, dtype=BF16):
    return jax.ShapeDtypeStruct(shape, dtype)


def iota(shape, dimension):
    return lax.broadcasted_iota(jnp.int32, shape, dimension)


def one_hot(condition):
    return jnp.where(condition, 1.0, 0.0).astype(BF16)


def dot(a, b, contract=(1, 0)):
    return lax.dot_general(a, b, (((contract[0],), (contract[1],)), ((), ())), preferred_element_type=F32)


def block_kernel(ids_ref, weights_ref, tokens_ref, out_ref):
    tokens, width = tokens_ref.shape
    lane = iota((tokens, LANES), 1)
    expert = lane & (N_Y * N_Z - 1)
    hits = jnp.zeros((tokens, LANES), F32)
    eighths = jnp.zeros((tokens, LANES), F32)
    weights = weights_ref[...].astype(F32)
    for choice in range(ids_ref.shape[1]):
        named = ids_ref[:, choice : choice + 1] == expert
        hits = hits + jnp.where(named, 1.0, 0.0)
        eighths = eighths + jnp.where(named, weights[:, choice : choice + 1], 0.0)
    earlier = one_hot(iota((tokens, tokens), 1) < iota((tokens, tokens), 0))
    rank = jnp.where(hits > 0.0, dot(earlier, hits.astype(BF16)), -1.0)
    out_ref[:, :width] = tokens_ref[...]
    out_ref[:, width:] = jnp.where(lane < N_Y * N_Z, rank, eighths).astype(BF16)


def slots_of(routing, expert, slot):
    lane = iota((LANES, expert.shape[1]), 0)
    rank = dot(routing, one_hot(lane == expert))
    eighths = dot(routing, one_hot(lane == expert + N_Y * N_Z))
    here = rank == slot.astype(F32)
    return here, jnp.where(here, eighths, 0.0)


def message_kernel(sign, z_ref, map_ref, block_ref, first_ref, second_ref, third_ref, select_ref):
    width = first_ref.shape[1]
    expert = map_ref[0:1, :] + ((z_ref[0] + sign * map_ref[1:2, :] + N_Z) & (N_Z - 1))
    here, eighths = slots_of(block_ref[:, width:], expert, map_ref[2:3, :])
    select = one_hot(here)
    select_ref[...] = select
    picked = dot(select, block_ref[:, :width], (0, 0))
    weights = jnp.sum(eighths, axis=0, keepdims=True)
    first = 0
    for ref, rows, slots in zip((first_ref, second_ref, third_ref), MESSAGE, MESSAGE_SLOTS):
        part = picked[first : first + rows]
        ref[...] = part.astype(BF16)
        is_weights = iota((rows, LANES), 0) == slots
        ref[:, :LANES] = jnp.where(is_weights, weights, part[:, :LANES]).astype(BF16)
        first += rows


def pick_kernel(blocks, z_ref, map_ref, *refs):
    messages = refs[blocks + 1 : -2] if len(refs) > blocks + 2 else ()
    out_ref, select_ref = refs[-2:]
    rows, width = out_ref.shape
    tokens = refs[0].shape[0]
    routing = jnp.concatenate([ref[:, width:] for ref in refs[:blocks]], axis=0)
    here, eighths = slots_of(routing, map_ref[0:1, :] + z_ref[0], map_ref[1:2, :])
    here = here & ((iota(here.shape, 0) >> (tokens.bit_length() - 1)) == map_ref[2:3, :])
    select = one_hot(here)
    select_ref[...] = select
    weights = jnp.sum(jnp.where(here, eighths, 0.0), axis=0, keepdims=True)
    picked = dot(select, jnp.concatenate([ref[:, :width] for ref in refs[:blocks]], axis=0), (0, 0))
    for index, ref in enumerate(messages):
        place_ref = refs[blocks]
        count = ref.shape[0]
        picked = picked + dot(one_hot(iota((rows, count), 1) == place_ref[:, index : index + 1]), ref[...])
        line = (index // 2) if index < 4 else 2
        spread = one_hot(iota((LANES, rows), 0) == map_ref[3 + index : 4 + index, :])
        lines = dot(ref[:, :LANES], spread)
        weights = weights + jnp.sum(
            jnp.where(iota(lines.shape, 0) == MESSAGE_SLOTS[line], lines, 0.0), axis=0, keepdims=True
        )
    out_ref[...] = picked.astype(BF16)
    used = (rows // N_Y - 1) // SLOTS * SLOTS
    row = iota((rows, rows), 0)
    is_weights = row == used
    for y in range(1, N_Y):
        is_weights = is_weights | (row == used + y * (rows // N_Y))
    out_ref[:, :rows] = jnp.where(is_weights, weights, picked[:, :rows]).astype(BF16)


MESSAGE_KEYS = tuple((step, way) for step in range(3) for way in range(2))


def message_map():
    maps = np.full((2, 8, MESSAGE_ROWS), -5, np.int32)
    for way in range(2):
        for step in range(3):
            for place in range(MESSAGE_SLOTS[step]):
                row = sum(MESSAGE[:step]) + place
                y = place // SLOTS + (2 if step == 2 and way == 1 else 0)
                maps[way, :3, row] = y * N_Z, step + 1, place % SLOTS
    return maps


def row_maps(sources, rows_of_y, blocks):
    rows = N_Y * rows_of_y
    lanes = np.full((16, rows), -5, np.int32)
    places = np.full((rows, 8), -5, np.int32)
    origin = np.full((3, rows), -1, np.int32)
    for y in range(N_Y):
        for index, source in enumerate(sources):
            for slot in range(SLOTS):
                row = y * rows_of_y + index * SLOTS + slot
                origin[:, row] = y, source, slot
                if index < blocks:
                    lanes[:3, row] = y * N_Z, slot, index
                    continue
                step = abs(source) - REACH - 1
                way = (y // 2) if step == 2 else (0 if source < 0 else 1)
                place = (y % 2 if step == 2 else y) * SLOTS + slot
                key = MESSAGE_KEYS.index((step, way))
                lanes[3 + key, row] = sum(MESSAGE[:step]) + place
                places[row, key] = place
    return lanes, places, origin


def part_kernel(place_ref, grads_ref, *out_refs):
    for index, ref in enumerate(out_refs):
        move = one_hot(iota((grads_ref.shape[0], ref.shape[0]), 1) == place_ref[:, index : index + 1])
        ref[...] = dot(move, grads_ref[...], (0, 0)).astype(BF16)


def relative_kernel(row_ref, values_ref, out_ref):
    move = one_hot(iota((row_ref.shape[0], values_ref.shape[0]), 1) == row_ref[...])
    out_ref[...] = dot(move, values_ref[...]).astype(BF16)


def absolute_kernel(row_ref, near_ref, last_ref, out_ref):
    move = one_hot(iota((row_ref.shape[0], out_ref.shape[0]), 1) == row_ref[...])
    count = near_ref.shape[0]
    out = dot(move[:count], near_ref[...], (0, 0)) + dot(move[count:], last_ref[...], (0, 0))
    out_ref[...] = out.astype(BF16)


def expert_kernel(y_ref, rows_ref, matrix_ref, cotangent_ref, hidden_ref, grad_ref, row_grads_ref):
    rows = rows_ref.shape[0]
    of_y = rows // N_Y
    units = hidden_ref.shape[1]
    row, lane = iota((rows, rows), 0), iota((rows, rows), 1)
    first = jnp.zeros((rows, rows), jnp.int32)
    for y in range(1, N_Y):
        first = jnp.where(row >= y * of_y, y * of_y, first)
    used = (of_y - 1) // SLOTS * SLOTS
    eighths = dot(one_hot(lane == first + used), rows_ref[:, :rows])
    eighths = jnp.where(lane == row - first + y_ref[0] * of_y, eighths, 0.0)
    weight = jnp.sum(eighths, axis=1, keepdims=True) * 0.125

    pre = dot(rows_ref[...], matrix_ref[...])
    gate_pre, up_pre = pre[:, :units], pre[:, units:]
    sigmoid_gate = jax.nn.sigmoid(gate_pre)
    activation = gate_pre * sigmoid_gate
    hidden_ref[...] = (activation * up_pre * weight).astype(BF16)
    act_slope = sigmoid_gate * (1.0 + gate_pre * (1.0 - sigmoid_gate))
    scaled = cotangent_ref[...].astype(F32) * weight
    grad_ref[:, :units] = (scaled * up_pre * act_slope).astype(BF16)
    grad_ref[:, units:] = (scaled * activation).astype(BF16)
    row_grads_ref[...] = dot(grad_ref[...], matrix_ref[...], (1, 1)).astype(BF16)


def meet_kernel(first_ref, second_ref, third_ref, messages_ref, grads_ref, own_ref, out_ref):
    rows = jnp.concatenate((first_ref[...], second_ref[...], third_ref[...]), axis=0)
    out_ref[...] = (dot(messages_ref[...], rows) + dot(own_ref[...], grads_ref[...])).astype(BF16)


def pass_kernel(sum_ref, grads_ref, own_ref, out_ref):
    out_ref[...] = (sum_ref[...].astype(F32) + dot(own_ref[...], grads_ref[...])).astype(BF16)


def end_kernel(up_ref, down_ref, grads_ref, own_ref, out_ref):
    out_ref[...] = up_ref[...].astype(F32) + down_ref[...].astype(F32) + dot(own_ref[...], grads_ref[...])


def call_block(kernel, out_shape, index, tokens, *operands):
    whole = pl.BlockSpec(memory_space=pltpu.VMEM)
    rows = operands[-1].shape[1]
    part = pl.BlockSpec((tokens, rows), lambda step: (index, 0))
    out_block = pl.BlockSpec(out_shape.shape, lambda step: (0, 0))
    return pl.pallas_call(
        kernel,
        grid=(1,),
        out_shape=out_shape,
        in_specs=[whole] * (len(operands) - 1) + [part],
        out_specs=out_block,
        compiler_params=pltpu.CompilerParams(vmem_limit_bytes=VMEM_BYTES),
    )(*operands)


def after(value, *others):
    return lax.optimization_barrier((value,) + others)[0]


def shards(tokens, expert_ids, route_weights, gate_weight, up_weight, cotangent):
    slot_count, units = cotangent.shape[2:]
    block, width = tokens.shape[1:]
    y, z = lax.axis_index("y").astype(jnp.int32), lax.axis_index("z").astype(jnp.int32)
    y_of, z_of = y.reshape(1), z.reshape(1)
    near_lanes, _, near_origin = row_maps(NEAR, NEAR_ROWS, len(NEAR))
    last_lanes, last_places, last_origin = row_maps(LAST, LAST_ROWS, 2)
    near_count, last_count = N_Y * NEAR_ROWS, N_Y * LAST_ROWS

    def send(value, distance):
        return lax.ppermute(value, "z", [(i, (i + distance) % N_Z) for i in range(N_Z)])

    def exchange(rows):
        parts = rows.reshape(N_Y, rows.shape[0] // N_Y, width)
        return lax.all_to_all(parts, "y", 0, 0, tiled=True).reshape(rows.shape)

    own = call(block_kernel, array((block, width + LANES)), expert_ids[0], route_weights[0], tokens[0])
    stacked = jnp.concatenate((gate_weight[0], up_weight[0]), axis=1)
    matrix = lax.all_gather(stacked, "dp", axis=0, tiled=True)

    group, offset, slot = np.concatenate((near_origin, last_origin), axis=1)
    row_of = ((group * N_Z + (z + offset + N_Z) % N_Z) * SLOTS + slot).astype(jnp.int32)
    row_of = jnp.where(group >= 0, row_of, -1)[:, None]
    cotangent_rows = call(relative_kernel, array((near_count + last_count, units)), row_of, cotangent[0, 0])

    blocks = {0: own}
    going = [own, own]
    for hop in range(1, REACH + 1):
        going = [send(going[0], 1), send(going[1], -1)]
        blocks[-hop], blocks[hop] = going
        if hop == REACH - 1:
            near_rows, near_select = call(
                functools.partial(pick_kernel, len(NEAR)),
                (array((near_count, width)), array((len(NEAR) * block, near_count))),
                z_of,
                jnp.asarray(near_lanes),
                *[blocks[source] for source in NEAR],
                scalars=1,
            )
    going = [after(part, near_rows) for part in going]
    near_rows = exchange(near_rows)
    messages = [
        call(
            functools.partial(message_kernel, sign),
            tuple(array((rows, width)) for rows in MESSAGE) + (array((block, MESSAGE_ROWS)),),
            z_of,
            jnp.asarray(message_map()[way]),
            going[way],
            scalars=1,
        )
        for way, sign in enumerate((1, -1))
    ]
    arrived = [send(messages[way][step], (step + 1) * (1 - 2 * way)) for step, way in MESSAGE_KEYS]
    last_rows, last_select = call(
        functools.partial(pick_kernel, 2),
        (array((last_count, width)), array((2 * block, last_count))),
        z_of,
        jnp.asarray(last_lanes),
        *[blocks[source] for source in LAST[:2]],
        jnp.asarray(last_places),
        *arrived,
        scalars=1,
    )
    last_rows = exchange(last_rows)

    def expert(rows, first):
        count = rows.shape[0]
        return call(
            expert_kernel,
            (array((count, units)), array((count, 2 * units)), array((count, width))),
            y_of,
            rows,
            matrix,
            cotangent_rows[first : first + count],
            scalars=1,
        )

    near_hidden, near_grads, near_back = expert(near_rows, 0)
    last_hidden, last_grads, last_back = expert(last_rows, near_count)
    near_terms = after(near_rows, last_grads)
    terms = (dot(near_terms, near_grads, (0, 0)) + dot(last_rows, last_grads, (0, 0))).astype(BF16)
    weight_grads = lax.psum_scatter(terms, "dp", scatter_dimension=0, tiled=True).astype(F32)
    gate_grads, up_grads = weight_grads[None, :, :units], weight_grads[None, :, units:]

    last_back = exchange(last_back)
    parts = call(
        part_kernel,
        tuple(array((MESSAGE[step], width)) for step, _ in MESSAGE_KEYS),
        jnp.asarray(last_places),
        last_back,
    )
    near_back = exchange(after(near_back, parts[0]))
    hidden = call(
        absolute_kernel, array((slot_count, units)), row_of, after(near_hidden, parts[0]), last_hidden
    )
    arrived = {
        key: send(part, -(key[0] + 1) * (1 - 2 * key[1])) for key, part in zip(MESSAGE_KEYS, parts)
    }
    whole = array((block, width))
    going = [
        call_block(
            meet_kernel,
            whole,
            LAST.index(REACH * (2 * way - 1)),
            block,
            *[arrived[step, way] for step in range(3)],
            messages[way][3],
            last_back,
            last_select,
        )
        for way in range(2)
    ]
    for hop in range(REACH - 1, -1, -1):
        going = [send(going[0], -1), send(going[1], 1)]
        if hop:
            going = [
                call_block(
                    pass_kernel, whole, NEAR.index(hop * (2 * way - 1)), block, going[way], near_back, near_select
                )
                for way in range(2)
            ]
    going[0] = after(going[0], gate_grads, up_grads, hidden)
    token_grads = call_block(end_kernel, array((block, width), F32), 0, block, *going, near_back, near_select)
    return hidden[None, None], token_grads[None], gate_grads, up_grads


def solution(mesh):
    grid = Mesh(mesh.devices.reshape(mesh.shape["dp"], N_Y, N_Z), ("dp", "y", "z"))
    expert = ("y", "z")
    in_specs = (
        P("dp", expert, None),
        P("dp", expert, None),
        P("dp", expert, None),
        P(expert, "dp", None),
        P(expert, "dp", None),
        P("dp", expert, None, None),
    )
    out_specs = (
        P("dp", expert, None, None),
        P("dp", expert, None),
        P(expert, "dp", None),
        P(expert, "dp", None),
    )
    return jax.shard_map(shards, mesh=grid, in_specs=in_specs, out_specs=out_specs, check_vma=False)
```

```python
import functools

import jax
import jax.numpy as jnp
import numpy as np
from jax import lax
from jax.experimental import pallas as pl
from jax.experimental.pallas import tpu as pltpu
from jax.sharding import Mesh, PartitionSpec as P

N_Y = 4
N_Z = 16
DIRECT = 512
VMEM_BYTES = 48 * 1024 * 1024


def routing_kernel(ids_ref, weights_ref, out_ref):
    rows, tokens = out_ref.shape
    row = lax.broadcasted_iota(jnp.int32, (rows, tokens), 0)
    kind = row % 8
    device = row // 8
    expert = jnp.where(kind < N_Y, kind * N_Z + device % N_Z, device)
    hits = jnp.zeros((rows, tokens), jnp.float32)
    eighths = jnp.zeros((rows, tokens), jnp.float32)
    for choice in range(ids_ref.shape[0]):
        named = ids_ref[choice : choice + 1, :] == expert
        hits = hits + jnp.where(named, 1.0, 0.0)
        eighths = eighths + jnp.where(named, weights_ref[choice : choice + 1, :].astype(jnp.float32), 0.0)
    earlier = lax.broadcasted_iota(jnp.int32, (tokens, tokens), 0)
    later = lax.broadcasted_iota(jnp.int32, (tokens, tokens), 1)
    triangle = jnp.where(earlier < later, 1.0, 0.0).astype(jnp.bfloat16)
    rank = jnp.dot(hits.astype(jnp.bfloat16), triangle, preferred_element_type=jnp.float32)
    rank = jnp.where(hits > 0.0, rank, -1.0)
    out_ref[...] = jnp.where(kind <= N_Y, rank, eighths).astype(jnp.bfloat16)


def slot_matrix(slot_ref, part, part_slots, part_tokens):
    columns = slice(part * part_tokens, (part + 1) * part_tokens)
    slot = lax.broadcasted_iota(jnp.int32, (part_slots, part_tokens), 0) + part * part_slots
    return jnp.concatenate(
        [jnp.where(slot_ref[y : y + 1, columns] == slot, 1.0, 0.0).astype(jnp.bfloat16) for y in range(N_Y)],
        axis=0,
    )


def pick_kernel(parts, slot_ref, tokens_ref, out_ref):
    part_slots = out_ref.shape[1] // parts
    part_tokens = tokens_ref.shape[0] // parts
    for part in range(parts):
        select = slot_matrix(slot_ref, part, part_slots, part_tokens)
        picked = jnp.dot(
            select,
            tokens_ref[part * part_tokens : (part + 1) * part_tokens, :],
            preferred_element_type=jnp.float32,
        ).astype(jnp.bfloat16)
        for y in range(N_Y):
            out_ref[y, part * part_slots : (part + 1) * part_slots, :] = picked[
                y * part_slots : (y + 1) * part_slots, :
            ]


def add_kernel(parts, slot_ref, grads_ref, out_ref):
    part_slots = grads_ref.shape[1] // parts
    part_tokens = out_ref.shape[0] // parts
    for part in range(parts):
        select = slot_matrix(slot_ref, part, part_slots, part_tokens)
        rows = jnp.concatenate(
            [grads_ref[y, part * part_slots : (part + 1) * part_slots, :] for y in range(N_Y)], axis=0
        )
        out_ref[part * part_tokens : (part + 1) * part_tokens, :] = lax.dot_general(
            select, rows, (((0,), (0,)), ((), ())), preferred_element_type=jnp.float32
        ).astype(jnp.bfloat16)


def dot(a, b, contract=(1, 0)):
    return lax.dot_general(
        a, b, (((contract[0],), (contract[1],)), ((), ())), preferred_element_type=jnp.float32
    )


def direct_pick_kernel(rank_ref, expert_ref, place_ref, tokens_ref, out_ref, select_ref):
    rows = out_ref.shape[0]
    spread = lax.broadcasted_iota(jnp.int32, (rows, rank_ref.shape[0]), 1) == expert_ref[...]
    rank = dot(jnp.where(spread, 1.0, 0.0).astype(jnp.bfloat16), rank_ref[...])
    select = jnp.where(rank == place_ref[...].astype(jnp.float32), 1.0, 0.0).astype(jnp.bfloat16)
    select_ref[...] = select
    out_ref[...] = dot(select, tokens_ref[...]).astype(jnp.bfloat16)


def expert_kernel(
    direct_ref, rows_ref, matrix_ref, weight_ref, cotangent_ref, hidden_ref, grad_ref, row_grads_ref
):
    units = hidden_ref.shape[1]
    width = direct_ref.shape[1]
    pre = dot(direct_ref[...], matrix_ref[:width, :]) + dot(rows_ref[...], matrix_ref[width:, :])
    gate_pre, up_pre = pre[:, :units], pre[:, units:]
    weight = weight_ref[...]
    sigmoid_gate = jax.nn.sigmoid(gate_pre)
    activation = gate_pre * sigmoid_gate
    hidden_ref[...] = (activation * up_pre * weight).astype(jnp.bfloat16)
    act_slope = sigmoid_gate * (1.0 + gate_pre * (1.0 - sigmoid_gate))
    scaled = cotangent_ref[...].astype(jnp.float32) * weight
    grad_ref[:, :units] = (scaled * up_pre * act_slope).astype(jnp.bfloat16)
    grad_ref[:, units:] = (scaled * activation).astype(jnp.bfloat16)
    row_grads_ref[...] = dot(grad_ref[...], matrix_ref[width:, :], (1, 1)).astype(jnp.bfloat16)


def call(kernel, out_shape, *operands):
    whole = pl.BlockSpec(memory_space=pltpu.VMEM)
    return pl.pallas_call(
        kernel,
        out_shape=out_shape,
        in_specs=[whole] * len(operands),
        out_specs=jax.tree.map(lambda _: whole, out_shape),
        compiler_params=pltpu.CompilerParams(vmem_limit_bytes=VMEM_BYTES),
    )(*operands)


def array(shape):
    return jax.ShapeDtypeStruct(shape, jnp.bfloat16)


def after(value, *others):
    return lax.optimization_barrier((value,) + others)[0]


def shards(tokens, expert_ids, route_weights, gate_weight, up_weight, cotangent):
    experts = N_Y * N_Z
    groups = lax.axis_size("dp")
    slot_count, units = cotangent.shape[2:]
    capacity = slot_count // experts
    row_slots = N_Z * capacity
    block, model_width = tokens.shape[1:]
    width = model_width - DIRECT

    def exchange(rows):
        parts = rows.reshape(N_Y, row_slots, rows.shape[1])
        return lax.all_to_all(parts, "y", 0, 0, tiled=True).reshape(rows.shape)

    def exchange_direct(rows):
        parts = rows.reshape(experts, 8, capacity * DIRECT // 8)
        return lax.all_to_all(parts, ("y", "z"), 0, 0, tiled=True).reshape(rows.shape)

    gathered = lax.all_gather(tokens[0, :, DIRECT:], "z", axis=0, tiled=True)

    told = call(routing_kernel, array((experts * 8, block)), expert_ids[0].T, route_weights[0].T)
    told = told.reshape(experts, 8, block)
    heard = lax.all_to_all(told, ("y", "z"), 0, 0, tiled=True)
    own_row = lax.dynamic_slice_in_dim(heard, lax.axis_index("y") * N_Z, N_Z, axis=0)
    rank = jnp.transpose(own_row[:, :N_Y], (1, 0, 2)).astype(jnp.int32)
    base = capacity * jnp.arange(N_Z, dtype=jnp.int32)[None, :, None]
    slot_of = jnp.where(rank >= 0, rank + base, -1).reshape(N_Y, N_Z * block)
    places = jnp.arange(capacity, dtype=jnp.int32).astype(jnp.bfloat16)
    weight_col = jnp.sum(
        jnp.where(
            heard[:, N_Y, None, :] == places[None, :, None],
            heard[:, N_Y + 1, None, :].astype(jnp.float32),
            0.0,
        ),
        axis=2,
    ).reshape(slot_count, 1) / 8.0

    slots = np.arange(slot_count, dtype=np.int32)[:, None]
    direct, select = call(
        direct_pick_kernel,
        (array((slot_count, DIRECT)), array((slot_count, block))),
        told[:, N_Y],
        jnp.asarray(slots // capacity),
        jnp.asarray(slots % capacity),
        tokens[0, :, :DIRECT],
    )
    direct = exchange_direct(direct)

    stacked = jnp.concatenate((gate_weight[0], up_weight[0]), axis=1)
    matrix = lax.all_to_all(
        jnp.broadcast_to(stacked[None], (groups,) + stacked.shape), "dp", 0, 0, tiled=True
    ).reshape(model_width, 2 * units)

    picked = call(functools.partial(pick_kernel, 2), array((N_Y, row_slots, width)), slot_of, gathered)
    rows = exchange(picked.reshape(slot_count, width))
    hidden, grads, row_grads = call(
        expert_kernel,
        (array((slot_count, units)), array((slot_count, 2 * units)), array((slot_count, width))),
        direct,
        rows,
        matrix,
        weight_col,
        cotangent[0, 0],
    )

    returned = exchange(row_grads).reshape(N_Y, row_slots, width)
    sums = call(functools.partial(add_kernel, 2), array((N_Z * block, width)), slot_of, returned)
    token_grads = lax.psum_scatter(sums, "z", scatter_dimension=0, tiled=True).astype(jnp.float32)

    late_grads = after(grads, sums)
    direct_grads = dot(late_grads, matrix[:DIRECT], (1, 1)).astype(jnp.bfloat16)
    direct_grads = dot(select, exchange_direct(direct_grads), (0, 0))
    terms = jnp.concatenate(
        (
            dot(direct, late_grads, (0, 0)).astype(jnp.bfloat16),
            dot(rows, late_grads, (0, 0)).astype(jnp.bfloat16),
        ),
        axis=0,
    ).reshape(groups, model_width // groups, 2 * units)
    weight_grads = jnp.sum(lax.all_to_all(terms, "dp", 0, 0, tiled=True).astype(jnp.float32), axis=0)
    return (
        hidden[None, None],
        jnp.concatenate((direct_grads, token_grads), axis=1)[None],
        weight_grads[None, :, :units],
        weight_grads[None, :, units:],
    )


def solution(mesh):
    grid = Mesh(mesh.devices.reshape(mesh.shape["dp"], N_Y, N_Z), ("dp", "y", "z"))
    expert = ("y", "z")
    in_specs = (
        P("dp", expert, None),
        P("dp", expert, None),
        P("dp", expert, None),
        P(expert, "dp", None),
        P(expert, "dp", None),
        P("dp", expert, None, None),
    )
    out_specs = (
        P("dp", expert, None, None),
        P("dp", expert, None),
        P(expert, "dp", None),
        P(expert, "dp", None),
    )
    return jax.shard_map(shards, mesh=grid, in_specs=in_specs, out_specs=out_specs, check_vma=False)
```

```python
import functools

import jax
import jax.numpy as jnp
import numpy as np
from jax import lax
from jax.experimental import pallas as pl
from jax.experimental.pallas import tpu as pltpu
from jax.sharding import Mesh, PartitionSpec as P

N_Y = 4
N_Z = 16
SLOTS = 10
REACH = 5
NEAR = (0, 1, -1, 2, -2, 3, -3, 4, -4)
LAST = (5, -5, 6, 7, 8, -7, -6)
NEAR_ROWS = 96
LAST_ROWS = 72
MESSAGE = (48, 48, 32)
MESSAGE_SLOTS = (40, 40, 20)
MESSAGE_ROWS = sum(MESSAGE)
LANES = 128
VMEM_BYTES = 48 * 1024 * 1024
F32 = jnp.float32
BF16 = jnp.bfloat16


def call(kernel, out_shape, *operands, scalars=0):
    whole = pl.BlockSpec(memory_space=pltpu.VMEM)
    small = pl.BlockSpec(memory_space=pltpu.SMEM)
    return pl.pallas_call(
        kernel,
        out_shape=out_shape,
        in_specs=[small] * scalars + [whole] * (len(operands) - scalars),
        out_specs=jax.tree.map(lambda _: whole, out_shape),
        compiler_params=pltpu.CompilerParams(vmem_limit_bytes=VMEM_BYTES),
    )(*operands)


def array(shape, dtype=BF16):
    return jax.ShapeDtypeStruct(shape, dtype)


def iota(shape, dimension):
    return lax.broadcasted_iota(jnp.int32, shape, dimension)


def one_hot(condition):
    return jnp.where(condition, 1.0, 0.0).astype(BF16)


def dot(a, b, contract=(1, 0)):
    return lax.dot_general(a, b, (((contract[0],), (contract[1],)), ((), ())), preferred_element_type=F32)


def block_kernel(ids_ref, weights_ref, tokens_ref, out_ref):
    tokens, width = tokens_ref.shape
    line = iota((LANES, tokens), 0)
    expert = line & (N_Y * N_Z - 1)
    hits = jnp.zeros((LANES, tokens), F32)
    eighths = jnp.zeros((LANES, tokens), F32)
    weights = weights_ref[...].astype(F32)
    for choice in range(ids_ref.shape[0]):
        named = ids_ref[choice : choice + 1, :] == expert
        hits = hits + jnp.where(named, 1.0, 0.0)
        eighths = eighths + jnp.where(named, weights[choice : choice + 1, :], 0.0)
    earlier = one_hot(iota((tokens, tokens), 0) < iota((tokens, tokens), 1))
    rank = jnp.where(hits > 0.0, dot(hits.astype(BF16), earlier), -1.0)
    routing = jnp.where(line < N_Y * N_Z, rank, eighths).astype(BF16)
    same = one_hot(iota((LANES, LANES), 0) == iota((LANES, LANES), 1))
    out_ref[:, :width] = tokens_ref[...]
    out_ref[:, width:] = dot(routing, same, (0, 0)).astype(BF16)


def slots_of(routing, expert, slot):
    lane = iota((LANES, expert.shape[1]), 0)
    rank = dot(routing, one_hot(lane == expert))
    eighths = dot(routing, one_hot(lane == expert + N_Y * N_Z))
    here = rank == slot.astype(F32)
    return here, jnp.where(here, eighths, 0.0)


def message_kernel(sign, z_ref, map_ref, block_ref, first_ref, second_ref, third_ref, select_ref):
    width = first_ref.shape[1]
    expert = map_ref[0:1, :] + ((z_ref[0] + sign * map_ref[1:2, :] + N_Z) & (N_Z - 1))
    here, eighths = slots_of(block_ref[:, width:], expert, map_ref[2:3, :])
    select = one_hot(here)
    select_ref[...] = select
    picked = dot(select, block_ref[:, :width], (0, 0))
    weights = jnp.sum(eighths, axis=0, keepdims=True)
    first = 0
    for ref, rows, slots in zip((first_ref, second_ref, third_ref), MESSAGE, MESSAGE_SLOTS):
        part = picked[first : first + rows]
        ref[...] = part.astype(BF16)
        is_weights = iota((rows, LANES), 0) == slots
        ref[:, :LANES] = jnp.where(is_weights, weights, part[:, :LANES]).astype(BF16)
        first += rows


def pick_kernel(blocks, messages, z_ref, map_ref, *refs):
    token_refs, routing_refs, refs = refs[:blocks], refs[blocks : 2 * blocks], refs[2 * blocks :]
    out_ref, select_ref = refs[-2:]
    rows = out_ref.shape[0]
    tokens = token_refs[0].shape[0]
    first = pl.program_id(0) == 0

    @pl.when(first)
    def _():
        routing = jnp.concatenate([ref[...] for ref in routing_refs], axis=0)
        here, _ = slots_of(routing, map_ref[0:1, :] + z_ref[0], map_ref[1:2, :])
        here = here & ((iota(here.shape, 0) >> (tokens.bit_length() - 1)) == map_ref[2:3, :])
        select_ref[...] = one_hot(here)

    picked = dot(select_ref[...], jnp.concatenate([ref[...] for ref in token_refs], axis=0), (0, 0))
    for index in range(messages):
        place_ref, ref = refs[0], refs[1 + index]
        picked = picked + dot(one_hot(iota((rows, ref.shape[0]), 1) == place_ref[:, index : index + 1]), ref[...])
    out_ref[...] = picked.astype(BF16)

    @pl.when(first)
    def _():
        routing = jnp.concatenate([ref[...] for ref in routing_refs], axis=0)
        lane = iota((LANES, rows), 0)
        eighths = dot(routing, one_hot(lane == map_ref[0:1, :] + z_ref[0] + N_Y * N_Z))
        weights = jnp.sum(select_ref[...].astype(F32) * eighths, axis=0, keepdims=True)
        for index in range(messages):
            ref = refs[1 + index]
            lines = dot(ref[:, :LANES], one_hot(lane == map_ref[3 + index : 4 + index, :]))
            line = MESSAGE_SLOTS[index // 2]
            weights = weights + jnp.sum(
                jnp.where(iota(lines.shape, 0) == line, lines, 0.0), axis=0, keepdims=True
            )
        used = (rows // N_Y - 1) // SLOTS * SLOTS
        row = iota((rows, rows), 0)
        is_weights = row == used
        for y in range(1, N_Y):
            is_weights = is_weights | (row == used + y * (rows // N_Y))
        out_ref[:, :rows] = jnp.where(is_weights, weights, picked[:, :rows]).astype(BF16)


def pick(z_of, lanes, places, blocks, messages, width):
    rows, tokens, step = lanes.shape[1], blocks[0].shape[0], 512
    whole = lambda value: pl.BlockSpec(value.shape, lambda part: (0, 0))
    others = (jnp.asarray(places),) + tuple(messages) if messages else ()
    return pl.pallas_call(
        functools.partial(pick_kernel, len(blocks), len(messages)),
        grid=(width // step,),
        out_shape=(array((rows, width)), array((len(blocks) * tokens, rows))),
        in_specs=[pl.BlockSpec(memory_space=pltpu.SMEM), whole(lanes)]
        + [pl.BlockSpec((tokens, step), lambda part: (0, part))] * len(blocks)
        + [pl.BlockSpec((tokens, LANES), lambda part: (0, width // LANES))] * len(blocks)
        + [whole(value) for value in others[:1]]
        + [pl.BlockSpec((value.shape[0], step), lambda part: (0, part)) for value in others[1:]],
        out_specs=(
            pl.BlockSpec((rows, step), lambda part: (0, part)),
            pl.BlockSpec((len(blocks) * tokens, rows), lambda part: (0, 0)),
        ),
        compiler_params=pltpu.CompilerParams(vmem_limit_bytes=VMEM_BYTES),
    )(z_of, jnp.asarray(lanes), *blocks, *blocks, *others)


MESSAGE_KEYS = tuple((step, way) for step in range(3) for way in range(2))


def message_map():
    maps = np.full((2, 8, MESSAGE_ROWS), -5, np.int32)
    for way in range(2):
        for step in range(3):
            for place in range(MESSAGE_SLOTS[step]):
                row = sum(MESSAGE[:step]) + place
                y = place // SLOTS + (2 if step == 2 and way == 1 else 0)
                maps[way, :3, row] = y * N_Z, step + 1, place % SLOTS
    return maps


def row_maps(sources, rows_of_y, blocks):
    rows = N_Y * rows_of_y
    lanes = np.full((16, rows), -5, np.int32)
    places = np.full((rows, 8), -5, np.int32)
    origin = np.full((3, rows), -1, np.int32)
    for y in range(N_Y):
        for index, source in enumerate(sources):
            for slot in range(SLOTS):
                row = y * rows_of_y + index * SLOTS + slot
                origin[:, row] = y, source, slot
                if index < blocks:
                    lanes[:3, row] = y * N_Z, slot, index
                    continue
                step = abs(source) - REACH - 1
                way = (y // 2) if step == 2 else (0 if source < 0 else 1)
                place = (y % 2 if step == 2 else y) * SLOTS + slot
                key = MESSAGE_KEYS.index((step, way))
                lanes[3 + key, row] = sum(MESSAGE[:step]) + place
                places[row, key] = place
    return lanes, places, origin


def part_kernel(place_ref, grads_ref, *out_refs):
    for index, ref in enumerate(out_refs):
        move = one_hot(iota((grads_ref.shape[0], ref.shape[0]), 1) == place_ref[:, index : index + 1])
        ref[...] = dot(move, grads_ref[...], (0, 0)).astype(BF16)


def relative_kernel(row_ref, values_ref, out_ref):
    move = one_hot(iota((row_ref.shape[0], values_ref.shape[0]), 1) == row_ref[...])
    out_ref[...] = dot(move, values_ref[...]).astype(BF16)


def absolute_kernel(row_ref, near_ref, last_ref, out_ref):
    move = one_hot(iota((row_ref.shape[0], out_ref.shape[0]), 1) == row_ref[...])
    count = near_ref.shape[0]
    out = dot(move[:count], near_ref[...], (0, 0)) + dot(move[count:], last_ref[...], (0, 0))
    out_ref[...] = out.astype(BF16)


def expert_kernel(y_ref, rows_ref, matrix_ref, cotangent_ref, hidden_ref, grad_ref, row_grads_ref):
    rows = rows_ref.shape[0]
    of_y = rows // N_Y
    units = hidden_ref.shape[1]
    row, lane = iota((rows, rows), 0), iota((rows, rows), 1)
    first = jnp.zeros((rows, rows), jnp.int32)
    for y in range(1, N_Y):
        first = jnp.where(row >= y * of_y, y * of_y, first)
    used = (of_y - 1) // SLOTS * SLOTS
    eighths = dot(one_hot(lane == first + used), rows_ref[:, :rows])
    eighths = jnp.where(lane == row - first + y_ref[0] * of_y, eighths, 0.0)
    weight = jnp.sum(eighths, axis=1, keepdims=True) * 0.125

    pre = dot(rows_ref[...], matrix_ref[...])
    gate_pre, up_pre = pre[:, :units], pre[:, units:]
    sigmoid_gate = jax.nn.sigmoid(gate_pre)
    activation = gate_pre * sigmoid_gate
    hidden_ref[...] = (activation * up_pre * weight).astype(BF16)
    act_slope = sigmoid_gate * (1.0 + gate_pre * (1.0 - sigmoid_gate))
    scaled = cotangent_ref[...].astype(F32) * weight
    grad_ref[:, :units] = (scaled * up_pre * act_slope).astype(BF16)
    grad_ref[:, units:] = (scaled * activation).astype(BF16)
    row_grads_ref[...] = dot(grad_ref[...], matrix_ref[...], (1, 1)).astype(BF16)


def meet_kernel(first_ref, second_ref, third_ref, messages_ref, grads_ref, own_ref, out_ref):
    rows = jnp.concatenate((first_ref[...], second_ref[...], third_ref[...]), axis=0)
    out_ref[...] = (dot(messages_ref[...], rows) + dot(own_ref[...], grads_ref[...])).astype(BF16)


def pass_kernel(sum_ref, grads_ref, own_ref, out_ref):
    out_ref[...] = (sum_ref[...].astype(F32) + dot(own_ref[...], grads_ref[...])).astype(BF16)


def end_kernel(up_ref, down_ref, grads_ref, own_ref, out_ref):
    out_ref[...] = up_ref[...].astype(F32) + down_ref[...].astype(F32) + dot(own_ref[...], grads_ref[...])


def call_block(kernel, out_shape, index, tokens, *operands):
    whole = pl.BlockSpec(memory_space=pltpu.VMEM)
    rows = operands[-1].shape[1]
    part = pl.BlockSpec((tokens, rows), lambda step: (index, 0))
    out_block = pl.BlockSpec(out_shape.shape, lambda step: (0, 0))
    return pl.pallas_call(
        kernel,
        grid=(1,),
        out_shape=out_shape,
        in_specs=[whole] * (len(operands) - 1) + [part],
        out_specs=out_block,
        compiler_params=pltpu.CompilerParams(vmem_limit_bytes=VMEM_BYTES),
    )(*operands)


def after(value, *others):
    return lax.optimization_barrier((value,) + others)[0]


def shards(tokens, expert_ids, route_weights, gate_weight, up_weight, cotangent):
    slot_count, units = cotangent.shape[2:]
    block, width = tokens.shape[1:]
    y, z = lax.axis_index("y").astype(jnp.int32), lax.axis_index("z").astype(jnp.int32)
    y_of, z_of = y.reshape(1), z.reshape(1)
    near_lanes, _, near_origin = row_maps(NEAR, NEAR_ROWS, len(NEAR))
    last_lanes, last_places, last_origin = row_maps(LAST, LAST_ROWS, 2)
    near_count, last_count = N_Y * NEAR_ROWS, N_Y * LAST_ROWS

    def send(value, distance):
        return lax.ppermute(value, "z", [(i, (i + distance) % N_Z) for i in range(N_Z)])

    def exchange(rows):
        parts = rows.reshape(N_Y, rows.shape[0] // N_Y, width)
        return lax.all_to_all(parts, "y", 0, 0, tiled=True).reshape(rows.shape)

    own = call(block_kernel, array((block, width + LANES)), expert_ids[0].T, route_weights[0].T, tokens[0])
    stacked = jnp.concatenate((after(gate_weight[0], own), up_weight[0]), axis=1)
    matrix = lax.all_gather(stacked, "dp", axis=0, tiled=True)

    group, offset, slot = np.concatenate((near_origin, last_origin), axis=1)
    row_of = ((group * N_Z + (z + offset + N_Z) % N_Z) * SLOTS + slot).astype(jnp.int32)
    row_of = jnp.where(group >= 0, row_of, -1)[:, None]
    cotangent_rows = call(relative_kernel, array((near_count + last_count, units)), row_of, cotangent[0, 0])

    blocks = {0: own}
    going = [own, own]
    for hop in range(1, REACH + 1):
        going = [send(going[0], 1), send(going[1], -1)]
        blocks[-hop], blocks[hop] = going
        if hop == REACH - 1:
            near_rows, near_select = pick(
                z_of, near_lanes, None, [blocks[source] for source in NEAR], (), width
            )
    going = [after(part, near_rows) for part in going]
    near_rows = exchange(near_rows)
    messages = [
        call(
            functools.partial(message_kernel, sign),
            tuple(array((rows, width)) for rows in MESSAGE) + (array((block, MESSAGE_ROWS)),),
            z_of,
            jnp.asarray(message_map()[way]),
            going[way],
            scalars=1,
        )
        for way, sign in enumerate((1, -1))
    ]
    arrived = [send(messages[way][step], (step + 1) * (1 - 2 * way)) for step, way in MESSAGE_KEYS]
    arrived[0] = after(arrived[0], near_rows)
    last_rows, last_select = pick(
        z_of, last_lanes, last_places, [blocks[source] for source in LAST[:2]], arrived, width
    )
    last_rows = exchange(last_rows)

    def expert(rows, first):
        count = rows.shape[0]
        return call(
            expert_kernel,
            (array((count, units)), array((count, 2 * units)), array((count, width))),
            y_of,
            rows,
            matrix,
            cotangent_rows[first : first + count],
            scalars=1,
        )

    near_hidden, near_grads, near_back = expert(near_rows, 0)
    last_hidden, last_grads, last_back = expert(last_rows, near_count)
    near_terms = after(near_rows, last_grads)
    terms = (dot(near_terms, near_grads, (0, 0)) + dot(last_rows, last_grads, (0, 0))).astype(BF16)
    weight_grads = lax.psum_scatter(terms, "dp", scatter_dimension=0, tiled=True).astype(F32)
    gate_grads, up_grads = weight_grads[None, :, :units], weight_grads[None, :, units:]

    last_back = exchange(last_back)
    parts = call(
        part_kernel,
        tuple(array((MESSAGE[step], width)) for step, _ in MESSAGE_KEYS),
        jnp.asarray(last_places),
        last_back,
    )
    near_back = exchange(after(near_back, parts[0]))
    hidden = call(
        absolute_kernel, array((slot_count, units)), row_of, after(near_hidden, parts[0]), last_hidden
    )
    arrived = {
        key: send(part, -(key[0] + 1) * (1 - 2 * key[1])) for key, part in zip(MESSAGE_KEYS, parts)
    }
    whole = array((block, width))
    going = [
        call_block(
            meet_kernel,
            whole,
            LAST.index(REACH * (2 * way - 1)),
            block,
            *[arrived[step, way] for step in range(3)],
            messages[way][3],
            last_back,
            last_select,
        )
        for way in range(2)
    ]
    for hop in range(REACH - 1, -1, -1):
        going = [send(going[0], -1), send(going[1], 1)]
        if hop:
            going = [
                call_block(
                    pass_kernel, whole, NEAR.index(hop * (2 * way - 1)), block, going[way], near_back, near_select
                )
                for way in range(2)
            ]
    going[0] = after(going[0], gate_grads, up_grads, hidden)
    token_grads = call_block(end_kernel, array((block, width), F32), 0, block, *going, near_back, near_select)
    return hidden[None, None], token_grads[None], gate_grads, up_grads


def solution(mesh):
    grid = Mesh(mesh.devices.reshape(mesh.shape["dp"], N_Y, N_Z), ("dp", "y", "z"))
    expert = ("y", "z")
    in_specs = (
        P("dp", expert, None),
        P("dp", expert, None),
        P("dp", expert, None),
        P(expert, "dp", None),
        P(expert, "dp", None),
        P("dp", expert, None, None),
    )
    out_specs = (
        P("dp", expert, None, None),
        P("dp", expert, None),
        P(expert, "dp", None),
        P(expert, "dp", None),
    )
    return jax.shard_map(shards, mesh=grid, in_specs=in_specs, out_specs=out_specs, check_vma=False)
```

```python
import functools

import jax
import jax.numpy as jnp
import numpy as np
from jax import lax
from jax.experimental import pallas as pl
from jax.experimental.pallas import tpu as pltpu
from jax.sharding import Mesh, PartitionSpec as P

N_Y = 4
N_Z = 16
SLOTS = 10
REACH = 5
NEAR = (0, 1, -1, 2, -2, 3, -3, 4, -4)
LAST = (5, -5, 6, 7, 8, -7, -6)
NEAR_ROWS = 96
LAST_ROWS = 72
MESSAGE = (48, 48, 32)
MESSAGE_SLOTS = (40, 40, 20)
MESSAGE_ROWS = sum(MESSAGE)
LANES = 128
VMEM_BYTES = 48 * 1024 * 1024
F32 = jnp.float32
BF16 = jnp.bfloat16


def call(kernel, out_shape, *operands, scalars=0):
    whole = pl.BlockSpec(memory_space=pltpu.VMEM)
    small = pl.BlockSpec(memory_space=pltpu.SMEM)
    return pl.pallas_call(
        kernel,
        out_shape=out_shape,
        in_specs=[small] * scalars + [whole] * (len(operands) - scalars),
        out_specs=jax.tree.map(lambda _: whole, out_shape),
        compiler_params=pltpu.CompilerParams(vmem_limit_bytes=VMEM_BYTES),
    )(*operands)


def array(shape, dtype=BF16):
    return jax.ShapeDtypeStruct(shape, dtype)


def iota(shape, dimension):
    return lax.broadcasted_iota(jnp.int32, shape, dimension)


def one_hot(condition):
    return jnp.where(condition, 1.0, 0.0).astype(BF16)


def dot(a, b, contract=(1, 0)):
    return lax.dot_general(a, b, (((contract[0],), (contract[1],)), ((), ())), preferred_element_type=F32)


def block_kernel(ids_ref, weights_ref, tokens_ref, out_ref):
    tokens, width = tokens_ref.shape
    line = iota((LANES, tokens), 0)
    expert = line & (N_Y * N_Z - 1)
    hits = jnp.zeros((LANES, tokens), F32)
    eighths = jnp.zeros((LANES, tokens), F32)
    weights = weights_ref[...].astype(F32)
    for choice in range(ids_ref.shape[0]):
        named = ids_ref[choice : choice + 1, :] == expert
        hits = hits + jnp.where(named, 1.0, 0.0)
        eighths = eighths + jnp.where(named, weights[choice : choice + 1, :], 0.0)
    earlier = one_hot(iota((tokens, tokens), 0) < iota((tokens, tokens), 1))
    rank = jnp.where(hits > 0.0, dot(hits.astype(BF16), earlier), -1.0)
    routing = jnp.where(line < N_Y * N_Z, rank, eighths).astype(BF16)
    same = one_hot(iota((LANES, LANES), 0) == iota((LANES, LANES), 1))
    out_ref[:, :width] = tokens_ref[...]
    out_ref[:, width:] = dot(routing, same, (0, 0)).astype(BF16)


def slots_of(routing, expert, slot):
    lane = iota((LANES, expert.shape[1]), 0)
    rank = dot(routing, one_hot(lane == expert))
    eighths = dot(routing, one_hot(lane == expert + N_Y * N_Z))
    here = rank == slot.astype(F32)
    return here, jnp.where(here, eighths, 0.0)


def message_kernel(sign, z_ref, map_ref, block_ref, first_ref, second_ref, third_ref, select_ref):
    width = first_ref.shape[1]
    expert = map_ref[0:1, :] + ((z_ref[0] + sign * map_ref[1:2, :] + N_Z) & (N_Z - 1))
    here, eighths = slots_of(block_ref[:, width:], expert, map_ref[2:3, :])
    select = one_hot(here)
    select_ref[...] = select
    picked = dot(select, block_ref[:, :width], (0, 0))
    weights = jnp.sum(eighths, axis=0, keepdims=True)
    first = 0
    for ref, rows, slots in zip((first_ref, second_ref, third_ref), MESSAGE, MESSAGE_SLOTS):
        part = picked[first : first + rows]
        ref[...] = part.astype(BF16)
        is_weights = iota((rows, LANES), 0) == slots
        ref[:, :LANES] = jnp.where(is_weights, weights, part[:, :LANES]).astype(BF16)
        first += rows


def pick_kernel(blocks, messages, z_ref, row_ref, lane_ref, place_ref, *refs):
    arrays, refs = refs[: blocks + messages], refs[blocks + messages :]
    out_ref, select_ref, tokens_ref = refs[:3]
    message_refs, copied = refs[3:-1], refs[-1]
    rows, width = out_ref.shape
    tokens = arrays[0].shape[0]
    targets = [tokens_ref.at[pl.ds(index * tokens, tokens), :] for index in range(blocks)] + list(message_refs)
    copies = [
        pltpu.make_async_copy(source, target, copied.at[index])
        for index, (source, target) in enumerate(zip(arrays, targets))
    ]
    for copy in copies:
        copy.start()
    for copy in copies:
        copy.wait()

    routing = tokens_ref[:, width:]
    line, lane = iota((rows, LANES), 1), iota((LANES, rows), 0)
    expert = row_ref[:, 0:1] + z_ref[0]
    rank = dot(one_hot(line == expert), routing, (1, 1))
    here = (rank == row_ref[:, 1:2].astype(F32)) & ((iota(rank.shape, 1) >> 7) == row_ref[:, 2:3])
    picked = dot(one_hot(here), tokens_ref[:, :width])

    expert = lane_ref[0:1, :] + z_ref[0]
    rank = dot(routing, one_hot(lane == expert))
    here = (rank == lane_ref[1:2, :].astype(F32)) & ((iota(rank.shape, 0) >> 7) == lane_ref[2:3, :])
    select_ref[...] = one_hot(here)
    eighths = dot(routing, one_hot(lane == expert + N_Y * N_Z))
    weights = jnp.sum(jnp.where(here, eighths, 0.0), axis=0, keepdims=True)
    for index, ref in enumerate(message_refs):
        picked = picked + dot(one_hot(iota((rows, ref.shape[0]), 1) == place_ref[:, index : index + 1]), ref[...])
        lines = dot(ref[:, :LANES], one_hot(lane == lane_ref[3 + index : 4 + index, :]))
        slots = MESSAGE_SLOTS[index // 2]
        weights = weights + jnp.sum(jnp.where(iota(lines.shape, 0) == slots, lines, 0.0), axis=0, keepdims=True)
    out_ref[...] = picked.astype(BF16)
    used = (rows // N_Y - 1) // SLOTS * SLOTS
    row = iota((rows, rows), 0)
    is_weights = row == used
    for y in range(1, N_Y):
        is_weights = is_weights | (row == used + y * (rows // N_Y))
    out_ref[:, :rows] = jnp.where(is_weights, weights, picked[:, :rows]).astype(BF16)


def pick(z_of, lanes, places, blocks, messages, width):
    rows, tokens = lanes.shape[1], blocks[0].shape[0]
    vmem = pl.BlockSpec(memory_space=pltpu.VMEM)
    count = len(blocks) + len(messages)
    return pl.pallas_call(
        functools.partial(pick_kernel, len(blocks), len(messages)),
        out_shape=(array((rows, width)), array((len(blocks) * tokens, rows))),
        in_specs=[pl.BlockSpec(memory_space=pltpu.SMEM)]
        + [vmem] * 3
        + [pl.BlockSpec(memory_space=pltpu.HBM)] * count,
        out_specs=(vmem, vmem),
        scratch_shapes=[pltpu.VMEM((len(blocks) * tokens, blocks[0].shape[1]), BF16)]
        + [pltpu.VMEM(message.shape, BF16) for message in messages]
        + [pltpu.SemaphoreType.DMA((count,))],
        compiler_params=pltpu.CompilerParams(vmem_limit_bytes=VMEM_BYTES),
    )(
        z_of,
        jnp.asarray(np.ascontiguousarray(lanes[:8].T)),
        jnp.asarray(lanes),
        jnp.asarray(places),
        *blocks,
        *messages,
    )


MESSAGE_KEYS = tuple((step, way) for step in range(3) for way in range(2))


def message_map():
    maps = np.full((2, 8, MESSAGE_ROWS), -5, np.int32)
    for way in range(2):
        for step in range(3):
            for place in range(MESSAGE_SLOTS[step]):
                row = sum(MESSAGE[:step]) + place
                y = place // SLOTS + (2 if step == 2 and way == 1 else 0)
                maps[way, :3, row] = y * N_Z, step + 1, place % SLOTS
    return maps


def row_maps(sources, rows_of_y, blocks):
    rows = N_Y * rows_of_y
    lanes = np.full((16, rows), -5, np.int32)
    places = np.full((rows, 8), -5, np.int32)
    origin = np.full((3, rows), -1, np.int32)
    for y in range(N_Y):
        for index, source in enumerate(sources):
            for slot in range(SLOTS):
                row = y * rows_of_y + index * SLOTS + slot
                origin[:, row] = y, source, slot
                if index < blocks:
                    lanes[:3, row] = y * N_Z, slot, index
                    continue
                step = abs(source) - REACH - 1
                way = (y // 2) if step == 2 else (0 if source < 0 else 1)
                place = (y % 2 if step == 2 else y) * SLOTS + slot
                key = MESSAGE_KEYS.index((step, way))
                lanes[3 + key, row] = sum(MESSAGE[:step]) + place
                places[row, key] = place
    return lanes, places, origin


def part_kernel(place_ref, grads_ref, *out_refs):
    for index, ref in enumerate(out_refs):
        move = one_hot(iota((grads_ref.shape[0], ref.shape[0]), 1) == place_ref[:, index : index + 1])
        ref[...] = dot(move, grads_ref[...], (0, 0)).astype(BF16)


def relative_kernel(row_ref, values_ref, out_ref):
    move = one_hot(iota((row_ref.shape[0], values_ref.shape[0]), 1) == row_ref[...])
    out_ref[...] = dot(move, values_ref[...]).astype(BF16)


def absolute_kernel(row_ref, near_ref, last_ref, out_ref):
    move = one_hot(iota((row_ref.shape[0], out_ref.shape[0]), 1) == row_ref[...])
    count = near_ref.shape[0]
    out = dot(move[:count], near_ref[...], (0, 0)) + dot(move[count:], last_ref[...], (0, 0))
    out_ref[...] = out.astype(BF16)


def expert_kernel(y_ref, rows_ref, gate_ref, up_ref, cotangent_ref, hidden_ref, grad_ref, row_grads_ref):
    rows = rows_ref.shape[0]
    of_y = rows // N_Y
    units = hidden_ref.shape[1]
    row, lane = iota((rows, rows), 0), iota((rows, rows), 1)
    first = jnp.zeros((rows, rows), jnp.int32)
    for y in range(1, N_Y):
        first = jnp.where(row >= y * of_y, y * of_y, first)
    used = (of_y - 1) // SLOTS * SLOTS
    eighths = dot(one_hot(lane == first + used), rows_ref[:, :rows])
    eighths = jnp.where(lane == row - first + y_ref[0] * of_y, eighths, 0.0)
    weight = jnp.sum(eighths, axis=1, keepdims=True) * 0.125

    gate_pre, up_pre = dot(rows_ref[...], gate_ref[...]), dot(rows_ref[...], up_ref[...])
    sigmoid_gate = jax.nn.sigmoid(gate_pre)
    activation = gate_pre * sigmoid_gate
    hidden_ref[...] = (activation * up_pre * weight).astype(BF16)
    act_slope = sigmoid_gate * (1.0 + gate_pre * (1.0 - sigmoid_gate))
    scaled = cotangent_ref[...].astype(F32) * weight
    grad_gate = (scaled * up_pre * act_slope).astype(BF16)
    grad_up = (scaled * activation).astype(BF16)
    grad_ref[:, :units] = grad_gate
    grad_ref[:, units:] = grad_up
    row_grads = dot(grad_gate, gate_ref[...], (1, 1)) + dot(grad_up, up_ref[...], (1, 1))
    row_grads_ref[...] = row_grads.astype(BF16)


def meet_kernel(first_ref, second_ref, third_ref, messages_ref, grads_ref, own_ref, out_ref):
    rows = jnp.concatenate((first_ref[...], second_ref[...], third_ref[...]), axis=0)
    out_ref[...] = (dot(messages_ref[...], rows) + dot(own_ref[...], grads_ref[...])).astype(BF16)


def pass_kernel(sum_ref, grads_ref, own_ref, out_ref):
    out_ref[...] = (sum_ref[...].astype(F32) + dot(own_ref[...], grads_ref[...])).astype(BF16)


def end_kernel(up_ref, down_ref, grads_ref, own_ref, out_ref):
    out_ref[...] = up_ref[...].astype(F32) + down_ref[...].astype(F32) + dot(own_ref[...], grads_ref[...])


def call_block(kernel, out_shape, index, tokens, *operands):
    whole = pl.BlockSpec(memory_space=pltpu.VMEM)
    rows = operands[-1].shape[1]
    part = pl.BlockSpec((tokens, rows), lambda step: (index, 0))
    out_block = pl.BlockSpec(out_shape.shape, lambda step: (0, 0))
    return pl.pallas_call(
        kernel,
        grid=(1,),
        out_shape=out_shape,
        in_specs=[whole] * (len(operands) - 1) + [part],
        out_specs=out_block,
        compiler_params=pltpu.CompilerParams(vmem_limit_bytes=VMEM_BYTES),
    )(*operands)


def after(value, *others):
    return lax.optimization_barrier((value,) + others)[0]


def shards(tokens, expert_ids, route_weights, gate_weight, up_weight, cotangent):
    slot_count, units = cotangent.shape[2:]
    block, width = tokens.shape[1:]
    y, z = lax.axis_index("y").astype(jnp.int32), lax.axis_index("z").astype(jnp.int32)
    y_of, z_of = y.reshape(1), z.reshape(1)
    near_lanes, near_places, near_origin = row_maps(NEAR, NEAR_ROWS, len(NEAR))
    last_lanes, last_places, last_origin = row_maps(LAST, LAST_ROWS, 2)
    near_count, last_count = N_Y * NEAR_ROWS, N_Y * LAST_ROWS

    def send(value, distance):
        return lax.ppermute(value, "z", [(i, (i + distance) % N_Z) for i in range(N_Z)])

    def exchange(rows):
        parts = rows.reshape(N_Y, rows.shape[0] // N_Y, width)
        return lax.all_to_all(parts, "y", 0, 0, tiled=True).reshape(rows.shape)

    own = call(block_kernel, array((block, width + LANES)), expert_ids[0].T, route_weights[0].T, tokens[0])

    gate_matrix = lax.all_gather(gate_weight[0], "dp", axis=0, tiled=True)
    up_matrix = lax.all_gather(up_weight[0], "dp", axis=0, tiled=True)

    group, offset, slot = np.concatenate((near_origin, last_origin), axis=1)
    row_of = ((group * N_Z + (z + offset + N_Z) % N_Z) * SLOTS + slot).astype(jnp.int32)
    row_of = jnp.where(group >= 0, row_of, -1)[:, None]
    cotangent_rows = call(relative_kernel, array((near_count + last_count, units)), row_of, cotangent[0, 0])

    blocks = {0: own}
    going = [own, own]
    for hop in range(1, REACH + 1):
        going = [send(going[0], 1), send(going[1], -1)]
        blocks[-hop], blocks[hop] = going
        if hop == REACH - 1:
            near_rows, near_select = pick(
                z_of, near_lanes, near_places, [blocks[source] for source in NEAR], (), width
            )
    going = [after(part, near_rows) for part in going]
    near_rows = exchange(near_rows)
    messages = [
        call(
            functools.partial(message_kernel, sign),
            tuple(array((rows, width)) for rows in MESSAGE) + (array((block, MESSAGE_ROWS)),),
            z_of,
            jnp.asarray(message_map()[way]),
            going[way],
            scalars=1,
        )
        for way, sign in enumerate((1, -1))
    ]
    arrived = [send(messages[way][step], (step + 1) * (1 - 2 * way)) for step, way in MESSAGE_KEYS]
    arrived[0] = after(arrived[0], near_rows)
    last_rows, last_select = pick(
        z_of, last_lanes, last_places, [blocks[source] for source in LAST[:2]], arrived, width
    )
    last_rows = exchange(last_rows)

    def expert(rows, first):
        count = rows.shape[0]
        return call(
            expert_kernel,
            (array((count, units)), array((count, 2 * units)), array((count, width))),
            y_of,
            rows,
            gate_matrix,
            up_matrix,
            cotangent_rows[first : first + count],
            scalars=1,
        )

    near_hidden, near_grads, near_back = expert(near_rows, 0)
    last_hidden, last_grads, last_back = expert(after(last_rows, near_grads), near_count)

    last_back = exchange(last_back)
    parts = call(
        part_kernel,
        tuple(array((MESSAGE[step], width)) for step, _ in MESSAGE_KEYS),
        jnp.asarray(last_places),
        last_back,
    )
    near_back = exchange(after(near_back, parts[0]))
    hidden = call(
        absolute_kernel, array((slot_count, units)), row_of, after(near_hidden, parts[0]), last_hidden
    )
    arrived = {
        key: send(part, -(key[0] + 1) * (1 - 2 * key[1])) for key, part in zip(MESSAGE_KEYS, parts)
    }
    whole = array((block, width))
    going = [
        call_block(
            meet_kernel,
            whole,
            LAST.index(REACH * (2 * way - 1)),
            block,
            *[arrived[step, way] for step in range(3)],
            messages[way][3],
            last_back,
            last_select,
        )
        for way in range(2)
    ]
    for hop in range(REACH - 1, -1, -1):
        going = [send(going[0], -1), send(going[1], 1)]
        if hop:
            going = [
                call_block(
                    pass_kernel, whole, NEAR.index(hop * (2 * way - 1)), block, going[way], near_back, near_select
                )
                for way in range(2)
            ]
        if hop == REACH - 1:
            near_terms, last_terms = after(near_rows, *going), after(last_rows, *going)
            terms = (dot(near_terms, near_grads, (0, 0)) + dot(last_terms, last_grads, (0, 0))).astype(BF16)
            weight_grads = lax.psum_scatter(terms, "dp", scatter_dimension=0, tiled=True).astype(F32)
            gate_grads, up_grads = weight_grads[None, :, :units], weight_grads[None, :, units:]
    going[0] = after(going[0], gate_grads, up_grads, hidden)
    token_grads = call_block(end_kernel, array((block, width), F32), 0, block, *going, near_back, near_select)
    return hidden[None, None], token_grads[None], gate_grads, up_grads


def solution(mesh):
    grid = Mesh(mesh.devices.reshape(mesh.shape["dp"], N_Y, N_Z), ("dp", "y", "z"))
    expert = ("y", "z")
    in_specs = (
        P("dp", expert, None),
        P("dp", expert, None),
        P("dp", expert, None),
        P(expert, "dp", None),
        P(expert, "dp", None),
        P("dp", expert, None, None),
    )
    out_specs = (
        P("dp", expert, None, None),
        P("dp", expert, None),
        P(expert, "dp", None),
        P(expert, "dp", None),
    )
    return jax.shard_map(shards, mesh=grid, in_specs=in_specs, out_specs=out_specs, check_vma=False)
```

```python
import functools

import jax
import jax.numpy as jnp
from jax import lax
from jax.experimental import pallas as pl
from jax.experimental.pallas import tpu as pltpu
from jax.sharding import Mesh, PartitionSpec as P

N_Y = 4
N_Z = 16
HALVES = 2
STEP = 512
VMEM_BYTES = 48 * 1024 * 1024


def routing_kernel(ids_ref, weights_ref, out_ref):
    rows, tokens = out_ref.shape
    row = lax.broadcasted_iota(jnp.int32, (rows, tokens), 0)
    kind = row % 8
    device = row // 8
    expert = jnp.where(kind < N_Y, kind * N_Z + device % N_Z, device)
    hits = jnp.zeros((rows, tokens), jnp.float32)
    eighths = jnp.zeros((rows, tokens), jnp.float32)
    for choice in range(ids_ref.shape[0]):
        named = ids_ref[choice : choice + 1, :] == expert
        hits = hits + jnp.where(named, 1.0, 0.0)
        eighths = eighths + jnp.where(named, weights_ref[choice : choice + 1, :].astype(jnp.float32), 0.0)
    earlier = lax.broadcasted_iota(jnp.int32, (tokens, tokens), 0)
    later = lax.broadcasted_iota(jnp.int32, (tokens, tokens), 1)
    triangle = jnp.where(earlier < later, 1.0, 0.0).astype(jnp.bfloat16)
    rank = jnp.dot(hits.astype(jnp.bfloat16), triangle, preferred_element_type=jnp.float32)
    rank = jnp.where(hits > 0.0, rank, -1.0)
    out_ref[...] = jnp.where(kind <= N_Y, rank, eighths).astype(jnp.bfloat16)


def array(shape, dtype=jnp.bfloat16):
    return jax.ShapeDtypeStruct(shape, dtype)


def dot(a, b, contract=(1, 0)):
    return lax.dot_general(
        a, b, (((contract[0],), (contract[1],)), ((), ())), preferred_element_type=jnp.float32
    )


def one_hot(condition):
    return jnp.where(condition, 1.0, 0.0).astype(jnp.bfloat16)


PARAMS = pltpu.CompilerParams(vmem_limit_bytes=VMEM_BYTES)
WHOLE = pl.BlockSpec(memory_space=pltpu.VMEM)


def pick_kernel(half, slot_ref, tokens_ref, out_ref, select_ref):
    slots = out_ref.shape[1]
    tokens = tokens_ref.shape[0]

    @pl.when(pl.program_id(0) == 0)
    def _():
        slot = lax.broadcasted_iota(jnp.int32, (slots, tokens), 0) + half * slots
        for y in range(N_Y):
            select_ref[y * slots : (y + 1) * slots, :] = one_hot(slot_ref[y : y + 1, :] == slot)

    picked = dot(select_ref[...], tokens_ref[...]).astype(jnp.bfloat16)
    for y in range(N_Y):
        out_ref[y] = picked[y * slots : (y + 1) * slots]


def pick(half, slot_of, gathered, slots):
    tokens, width = gathered.shape[0] // HALVES, gathered.shape[1]
    return pl.pallas_call(
        functools.partial(pick_kernel, half),
        grid=(width // STEP,),
        out_shape=array((N_Y, slots, width)),
        in_specs=[
            pl.BlockSpec((N_Y, tokens), lambda step: (0, half)),
            pl.BlockSpec((tokens, STEP), lambda step: (half, step)),
        ],
        out_specs=pl.BlockSpec((N_Y, slots, STEP), lambda step: (0, 0, step)),
        scratch_shapes=[pltpu.VMEM((N_Y * slots, tokens), jnp.bfloat16)],
        compiler_params=PARAMS,
    )(slot_of, gathered)


def expert_kernel(
    rows_ref, matrix_ref, weight_ref, cotangent_ref, hidden_ref, grad_ref, row_grads_ref
):
    units = hidden_ref.shape[2]
    slots = hidden_ref.shape[1]
    pre = dot(rows_ref[...], matrix_ref[...])
    weights = jnp.concatenate([weight_ref[y] for y in range(N_Y)], axis=0)
    cotangent = jnp.concatenate([cotangent_ref[y] for y in range(N_Y)], axis=0)
    gate_pre, up_pre = pre[:, :units], pre[:, units:]
    sigmoid_gate = jax.nn.sigmoid(gate_pre)
    activation = gate_pre * sigmoid_gate
    hidden = (activation * up_pre * weights).astype(jnp.bfloat16)
    for y in range(N_Y):
        hidden_ref[y] = hidden[y * slots : (y + 1) * slots]
    act_slope = sigmoid_gate * (1.0 + gate_pre * (1.0 - sigmoid_gate))
    scaled = cotangent.astype(jnp.float32) * weights
    grad_ref[:, :units] = (scaled * up_pre * act_slope).astype(jnp.bfloat16)
    grad_ref[:, units:] = (scaled * activation).astype(jnp.bfloat16)
    row_grads_ref[...] = dot(grad_ref[...], matrix_ref[...], (1, 1)).astype(jnp.bfloat16)


def expert(half, rows, matrix, weight_col, cotangent):
    count, width = rows.shape
    slots, units = count // N_Y, cotangent.shape[2]
    return pl.pallas_call(
        expert_kernel,
        grid=(1,),
        out_shape=(array((N_Y, slots, units)), array((count, 2 * units)), array((count, width))),
        in_specs=[
            WHOLE,
            WHOLE,
            pl.BlockSpec((N_Y, slots, 1), lambda step: (0, half, 0)),
            pl.BlockSpec((N_Y, slots, units), lambda step: (0, half, 0)),
        ],
        out_specs=(
            pl.BlockSpec((N_Y, slots, units), lambda step: (0, 0, 0)),
            pl.BlockSpec((count, 2 * units), lambda step: (0, 0)),
            pl.BlockSpec((count, width), lambda step: (0, 0)),
        ),
        compiler_params=PARAMS,
    )(rows, matrix, weight_col, cotangent)


def add_kernel(half, place_ref, grads_ref, *refs):
    out_ref, select_ref = refs[-2:]
    tokens, rows = select_ref.shape
    slots = rows // N_Y

    @pl.when(pl.program_id(0) == 0)
    def _():
        row = lax.broadcasted_iota(jnp.int32, (tokens, rows), 1)
        mark = place_ref[:, 0:1] - half * slots == row
        mark = mark & (row < slots)
        for y in range(1, N_Y):
            here = place_ref[:, y : y + 1] + (y - half) * slots == row
            mark = mark | (here & (row >= y * slots) & (row < (y + 1) * slots))
        select_ref[...] = one_hot(mark)

    grads = jnp.concatenate([grads_ref[y] for y in range(N_Y)], axis=0)
    out_ref[...] = dot(select_ref[...], grads).astype(jnp.bfloat16)


def add(half, place_of, grads, earlier):
    slots, width = grads.shape[1:]
    count = place_of.shape[0]
    tokens = count // HALVES
    return pl.pallas_call(
        functools.partial(add_kernel, half),
        grid=(width // STEP,),
        out_shape=array((count, width)),
        in_specs=[
            pl.BlockSpec((tokens, N_Y), lambda step: (half, 0)),
            pl.BlockSpec((N_Y, slots, STEP), lambda step: (0, 0, step)),
        ]
        + [pl.BlockSpec(memory_space=pl.ANY)] * len(earlier),
        out_specs=pl.BlockSpec((tokens, STEP), lambda step: (half, step)),
        scratch_shapes=[pltpu.VMEM((tokens, N_Y * slots), jnp.bfloat16)],
        input_output_aliases={2: 0} if earlier else {},
        compiler_params=PARAMS,
    )(place_of, grads, *earlier)


def after(value, *others):
    return lax.optimization_barrier((value,) + others)[0]


def shards(tokens, expert_ids, route_weights, gate_weight, up_weight, cotangent):
    experts = N_Y * N_Z
    groups = lax.axis_size("dp")
    slot_count, units = cotangent.shape[2:]
    capacity = slot_count // experts
    row_slots = N_Z * capacity
    half_slots = row_slots // HALVES
    block, width = tokens.shape[1:]

    def exchange(parts):
        return lax.all_to_all(parts, "y", 0, 0, tiled=True)

    gathered = lax.all_gather(tokens[0], "z", axis=0, tiled=True)

    told = pl.pallas_call(
        routing_kernel,
        out_shape=array((experts * 8, block)),
        in_specs=[WHOLE, WHOLE],
        out_specs=WHOLE,
        compiler_params=PARAMS,
    )(expert_ids[0].T, route_weights[0].T)
    heard = lax.all_to_all(told.reshape(experts, 8, block), ("y", "z"), 0, 0, tiled=True)
    own_row = lax.dynamic_slice_in_dim(heard, lax.axis_index("y") * N_Z, N_Z, axis=0)
    rank = jnp.transpose(own_row[:, :N_Y], (1, 0, 2)).astype(jnp.int32)
    base = capacity * jnp.arange(N_Z, dtype=jnp.int32)[None, :, None]
    slot_of = jnp.where(rank >= 0, rank + base, -1).reshape(N_Y, N_Z * block)
    place_of = slot_of.T
    places = jnp.arange(capacity, dtype=jnp.int32).astype(jnp.bfloat16)
    weight_col = jnp.sum(
        jnp.where(
            heard[:, N_Y, None, :] == places[None, :, None],
            heard[:, N_Y + 1, None, :].astype(jnp.float32),
            0.0,
        ),
        axis=2,
    ).reshape(N_Y, row_slots, 1) / 8.0

    stacked = jnp.concatenate((gate_weight[0], up_weight[0]), axis=1)
    matrix = lax.all_to_all(
        jnp.broadcast_to(stacked[None], (groups,) + stacked.shape), "dp", 0, 0, tiled=True
    ).reshape(width, 2 * units)

    cotangents = cotangent.reshape(N_Y, row_slots, units)
    rows, hidden, grads, back = [], [], [], []
    for half in range(HALVES):
        arrived = exchange(pick(half, slot_of, gathered, half_slots)).reshape(N_Y * half_slots, width)
        results = expert(half, arrived, matrix, weight_col, cotangents)
        for known, result in zip((rows, hidden, grads, back), (arrived,) + tuple(results)):
            known.append(result)
    sums = ()
    for half in range(HALVES):
        own = after(back[half], rows[-1])
        returned = exchange(own.reshape(N_Y, half_slots, width))
        sums = (add(half, place_of, returned, sums),)
    token_grads = lax.psum_scatter(sums[0], "z", scatter_dimension=0, tiled=True).astype(jnp.float32)

    late_grads = [after(value, sums[0]) for value in grads]
    terms = sum(dot(value, grad, (0, 0)) for value, grad in zip(rows, late_grads)).astype(jnp.bfloat16)
    terms = terms.reshape(groups, width // groups, 2 * units)
    weight_grads = jnp.sum(lax.all_to_all(terms, "dp", 0, 0, tiled=True).astype(jnp.float32), axis=0)
    hidden = after(jnp.concatenate([after(value, sums[0]) for value in hidden], axis=1))
    return (
        hidden.reshape(cotangent.shape),
        token_grads[None],
        weight_grads[None, :, :units],
        weight_grads[None, :, units:],
    )


def solution(mesh):
    grid = Mesh(mesh.devices.reshape(mesh.shape["dp"], N_Y, N_Z), ("dp", "y", "z"))
    expert = ("y", "z")
    in_specs = (
        P("dp", expert, None),
        P("dp", expert, None),
        P("dp", expert, None),
        P(expert, "dp", None),
        P(expert, "dp", None),
        P("dp", expert, None, None),
    )
    out_specs = (
        P("dp", expert, None, None),
        P("dp", expert, None),
        P(expert, "dp", None),
        P(expert, "dp", None),
    )
    return jax.shard_map(shards, mesh=grid, in_specs=in_specs, out_specs=out_specs, check_vma=False)
```

```python
import functools

import jax
import jax.numpy as jnp
import numpy as np
from jax import lax
from jax.experimental import pallas as pl
from jax.experimental.pallas import tpu as pltpu
from jax.sharding import PartitionSpec as P

LINES = 8
QUARTERS = 4
LANES = 128
VMEM_BYTES = 48 * 1024 * 1024
F32 = jnp.float32
BF16 = jnp.bfloat16


def call(kernel, out_shape, *operands):
    whole = pl.BlockSpec(memory_space=pltpu.VMEM)
    return pl.pallas_call(
        kernel,
        out_shape=out_shape,
        in_specs=[whole] * len(operands),
        out_specs=jax.tree.map(lambda _: whole, out_shape),
        compiler_params=pltpu.CompilerParams(vmem_limit_bytes=VMEM_BYTES),
    )(*operands)


def array(shape, dtype=BF16):
    return jax.ShapeDtypeStruct(shape, dtype)


def iota(shape, dimension):
    return lax.broadcasted_iota(jnp.int32, shape, dimension)


def one_hot(condition):
    return jnp.where(condition, 1.0, 0.0).astype(BF16)


def dot(a, b, contract=(1, 0)):
    return lax.dot_general(a, b, (((contract[0],), (contract[1],)), ((), ())), preferred_element_type=F32)


def of_quarter(select, quarter):
    line = iota(select.shape, 0) & (LINES - 1)
    return jnp.where((line & (QUARTERS - 1)) == quarter, select, jnp.zeros_like(select))


def source_kernel(ids_ref, weights_ref, tokens_ref, out_ref, main_ref, extra_ref):
    tokens, width = tokens_ref.shape
    step = width // QUARTERS
    shape = (out_ref.shape[0], tokens)
    row = iota(shape, 0)
    expert, line = row // LINES, row & (LINES - 1)
    hits = jnp.zeros(shape, F32)
    eighths = jnp.zeros(shape, F32)
    weights = weights_ref[...].astype(F32)
    for choice in range(ids_ref.shape[0]):
        named = ids_ref[choice : choice + 1, :] == expert
        hits = hits + jnp.where(named, 1.0, 0.0)
        eighths = eighths + jnp.where(named, weights[choice : choice + 1, :], 0.0)
    earlier = one_hot(iota((tokens, tokens), 0) < iota((tokens, tokens), 1))
    rank = jnp.where(hits > 0.0, dot(hits.astype(BF16), earlier), -1.0).astype(jnp.int32)
    is_main = rank == line
    is_extra = rank == LINES + line // QUARTERS
    main, extra = one_hot(is_main), one_hot(is_extra)
    main_ref[...] = main
    extra_ref[...] = extra
    out_ref[:, :width] = dot(main, tokens_ref[...]).astype(BF16)
    beside = dot(of_quarter(extra, 0), tokens_ref[:, :step])
    for quarter in range(1, QUARTERS):
        beside = beside + dot(of_quarter(extra, quarter), tokens_ref[:, quarter * step : (quarter + 1) * step])
    out_ref[:, width : width + step] = beside.astype(BF16)
    main_weight = jnp.sum(jnp.where(is_main, eighths, 0.0), axis=1, keepdims=True)
    extra_weight = jnp.sum(jnp.where(is_extra, eighths, 0.0), axis=1, keepdims=True)
    lane = iota((shape[0], LANES), 1)
    both = jnp.where(lane == 0, main_weight, jnp.where(lane == 1, extra_weight, 0.0))
    out_ref[:, width + step :] = both.astype(BF16)


def order_of(sources):
    slots = LINES + 2
    first = [source * slots + slot for source in range(sources) for slot in range(LINES)]
    return np.array(first + [source * slots + slot for slot in (8, 9) for source in range(sources)], np.int32)


def reorder_kernel(row_ref, values_ref, out_ref):
    move = one_hot(iota((row_ref.shape[0], values_ref.shape[0]), 1) == row_ref[...])
    out_ref[...] = dot(move, values_ref[...]).astype(BF16)


def lines_of(rows, lines, quarter):
    row = iota((rows, lines), 0)
    sources = rows // 2
    source, second = row & (sources - 1), row // sources
    return one_hot(iota((rows, lines), 1) == source * LINES + second * QUARTERS + quarter)


def expert_kernel(
    blocks_ref, matrix_ref, cotangent_ref, row_ref, hidden_ref, grad_ref, extra_ref, back_ref
):
    lines, extras = blocks_ref.shape[0], extra_ref.shape[0]
    width = matrix_ref.shape[0]
    step = width // QUARTERS
    units = hidden_ref.shape[1]
    places = [lines_of(extras, lines, quarter) for quarter in range(QUARTERS)]
    beside = blocks_ref[:, width : width + step]
    for quarter in range(QUARTERS):
        extra_ref[:, quarter * step : (quarter + 1) * step] = dot(places[quarter], beside).astype(BF16)
    weights = blocks_ref[:, width + step :]
    main_weight = weights[:, 0:1].astype(F32)
    extra_weight = dot(places[0], weights)[:, 1:2]
    weight = jnp.concatenate((main_weight, extra_weight), axis=0) * 0.125

    pre = jnp.concatenate(
        (dot(blocks_ref[:, :width], matrix_ref[...]), dot(extra_ref[...], matrix_ref[...])), axis=0
    )
    gate_pre, up_pre = pre[:, :units], pre[:, units:]
    sigmoid_gate = jax.nn.sigmoid(gate_pre)
    activation = gate_pre * sigmoid_gate
    hidden = (activation * up_pre * weight).astype(BF16)
    act_slope = sigmoid_gate * (1.0 + gate_pre * (1.0 - sigmoid_gate))
    scaled = cotangent_ref[...].astype(F32) * weight
    grad_ref[:, :units] = (scaled * up_pre * act_slope).astype(BF16)
    grad_ref[:, units:] = (scaled * activation).astype(BF16)
    back_ref[:, :width] = dot(grad_ref[:lines, :], matrix_ref[...], (1, 1)).astype(BF16)
    extra_back = dot(grad_ref[lines:, :], matrix_ref[...], (1, 1)).astype(BF16)
    beside = dot(places[0], extra_back[:, :step], (0, 0))
    for quarter in range(1, QUARTERS):
        beside = beside + dot(places[quarter], extra_back[:, quarter * step : (quarter + 1) * step], (0, 0))
    back_ref[:, width:] = beside.astype(BF16)
    move = one_hot(iota((row_ref.shape[0], hidden.shape[0]), 1) == row_ref[...])
    hidden_ref[...] = dot(move, hidden).astype(BF16)


def token_kernel(main_ref, extra_ref, blocks_ref, out_ref):
    width = out_ref.shape[1]
    step = width // QUARTERS
    extra = extra_ref[...]
    total = dot(main_ref[...], blocks_ref[:, :width], (0, 0))
    for quarter in range(QUARTERS):
        part = slice(quarter * step, (quarter + 1) * step)
        out_ref[:, part] = total[:, part] + dot(of_quarter(extra, quarter), blocks_ref[:, width:], (0, 0))


def shards(tokens, expert_ids, route_weights, gate_weight, up_weight, cotangent):
    experts = lax.axis_size("expert")
    slot_count, units = cotangent.shape[2:]
    block, width = tokens.shape[1:]
    lines, extras = experts * LINES, experts * 2
    step = width // QUARTERS

    def exchange(blocks):
        parts = blocks.reshape(experts, LINES, blocks.shape[1])
        return lax.all_to_all(parts, "expert", 0, 0, tiled=True).reshape(blocks.shape)

    outgoing, main, extra = call(
        source_kernel,
        (array((lines, width + step + LANES)), array((lines, block)), array((lines, block))),
        expert_ids[0].T,
        route_weights[0].T,
        tokens[0],
    )
    arrived = exchange(outgoing)

    stacked = jnp.concatenate((gate_weight[0], up_weight[0]), axis=1)
    matrix = lax.all_gather(stacked, "dp", axis=0, tiled=True)
    order = order_of(experts)
    cotangent_rows = call(
        reorder_kernel, array((slot_count, units)), jnp.asarray(order[:, None]), cotangent[0, 0]
    )
    hidden, grads, extra_rows, back = call(
        expert_kernel,
        (
            array((slot_count, units)),
            array((slot_count, 2 * units)),
            array((extras, width)),
            array((lines, width + step)),
        ),
        arrived,
        matrix,
        cotangent_rows,
        jnp.asarray(np.argsort(order).astype(np.int32)[:, None]),
    )
    token_grads = call(token_kernel, array((block, width), F32), main, extra, exchange(back))

    terms = dot(arrived[:, :width], grads[:lines], (0, 0)) + dot(extra_rows, grads[lines:], (0, 0))
    weight_grads = lax.psum_scatter(terms.astype(BF16), "dp", scatter_dimension=0, tiled=True).astype(F32)
    return (
        hidden[None, None],
        token_grads[None],
        weight_grads[None, :, :units],
        weight_grads[None, :, units:],
    )


def solution(mesh):
    in_specs = (
        P("dp", "expert", None),
        P("dp", "expert", None),
        P("dp", "expert", None),
        P("expert", "dp", None),
        P("expert", "dp", None),
        P("dp", "expert", None, None),
    )
    out_specs = (
        P("dp", "expert", None, None),
        P("dp", "expert", None),
        P("expert", "dp", None),
        P("expert", "dp", None),
    )
    return jax.shard_map(shards, mesh=mesh, in_specs=in_specs, out_specs=out_specs, check_vma=False)
```

```python
import functools

import jax
import jax.numpy as jnp
import numpy as np
from jax import lax
from jax.experimental import pallas as pl
from jax.experimental.pallas import tpu as pltpu
from jax.sharding import Mesh, PartitionSpec as P

N_Y = 4
N_Z = 16
DIRECT = 512
HALVES = 2
STEP = 512
VMEM_BYTES = 48 * 1024 * 1024


def routing_kernel(ids_ref, weights_ref, out_ref):
    rows, tokens = out_ref.shape
    row = lax.broadcasted_iota(jnp.int32, (rows, tokens), 0)
    kind = row % 8
    device = row // 8
    expert = jnp.where(kind < N_Y, kind * N_Z + device % N_Z, device)
    hits = jnp.zeros((rows, tokens), jnp.float32)
    eighths = jnp.zeros((rows, tokens), jnp.float32)
    for choice in range(ids_ref.shape[0]):
        named = ids_ref[choice : choice + 1, :] == expert
        hits = hits + jnp.where(named, 1.0, 0.0)
        eighths = eighths + jnp.where(named, weights_ref[choice : choice + 1, :].astype(jnp.float32), 0.0)
    earlier = lax.broadcasted_iota(jnp.int32, (tokens, tokens), 0)
    later = lax.broadcasted_iota(jnp.int32, (tokens, tokens), 1)
    triangle = jnp.where(earlier < later, 1.0, 0.0).astype(jnp.bfloat16)
    rank = jnp.dot(hits.astype(jnp.bfloat16), triangle, preferred_element_type=jnp.float32)
    rank = jnp.where(hits > 0.0, rank, -1.0)
    out_ref[...] = jnp.where(kind <= N_Y, rank, eighths).astype(jnp.bfloat16)


def array(shape, dtype=jnp.bfloat16):
    return jax.ShapeDtypeStruct(shape, dtype)


def dot(a, b, contract=(1, 0)):
    return lax.dot_general(
        a, b, (((contract[0],), (contract[1],)), ((), ())), preferred_element_type=jnp.float32
    )


def one_hot(condition):
    return jnp.where(condition, 1.0, 0.0).astype(jnp.bfloat16)


PARAMS = pltpu.CompilerParams(vmem_limit_bytes=VMEM_BYTES)
WHOLE = pl.BlockSpec(memory_space=pltpu.VMEM)


def direct_pick_kernel(rank_ref, expert_ref, place_ref, tokens_ref, out_ref, select_ref):
    rows = out_ref.shape[0]
    spread = lax.broadcasted_iota(jnp.int32, (rows, rank_ref.shape[0]), 1) == expert_ref[...]
    rank = dot(jnp.where(spread, 1.0, 0.0).astype(jnp.bfloat16), rank_ref[...])
    select = jnp.where(rank == place_ref[...].astype(jnp.float32), 1.0, 0.0).astype(jnp.bfloat16)
    select_ref[...] = select
    out_ref[...] = dot(select, tokens_ref[...]).astype(jnp.bfloat16)


def select_kernel(slot_ref, place_ref, pick_ref, add_ref):
    halves, rows, tokens = pick_ref.shape
    slots = rows // N_Y
    for half in range(halves):
        part = slice(half * tokens, (half + 1) * tokens)
        slot = lax.broadcasted_iota(jnp.int32, (slots, tokens), 0) + half * slots
        for y in range(N_Y):
            pick_ref[half, y * slots : (y + 1) * slots, :] = one_hot(slot_ref[y : y + 1, part] == slot)
        row = lax.broadcasted_iota(jnp.int32, (tokens, rows), 1)
        mark = (place_ref[part, 0:1] - half * slots == row) & (row < slots)
        for y in range(1, N_Y):
            here = place_ref[part, y : y + 1] + (y - half) * slots == row
            mark = mark | (here & (row >= y * slots) & (row < (y + 1) * slots))
        add_ref[half] = one_hot(mark)


def pick_kernel(select_ref, tokens_ref, *out_refs):
    halves, rows, tokens = select_ref.shape
    slots = rows // N_Y
    for half in range(halves):
        part = tokens_ref[half * tokens : (half + 1) * tokens, :]
        picked = dot(select_ref[half], part).astype(jnp.bfloat16)
        for y, out_ref in enumerate(out_refs):
            out_ref[half * slots : (half + 1) * slots, :] = picked[y * slots : (y + 1) * slots]


def add_kernel(select_ref, *refs):
    grad_refs, out_ref = refs[:-1], refs[-1]
    halves, tokens, rows = select_ref.shape
    slots = rows // N_Y
    for half in range(halves):
        part = slice(half * slots, (half + 1) * slots)
        grads = jnp.concatenate([ref[part, :] for ref in grad_refs], axis=0)
        out_ref[half * tokens : (half + 1) * tokens, :] = dot(select_ref[half], grads).astype(jnp.bfloat16)


def by_columns(kernel, out_shapes, select, *values):
    def part(rows):
        return pl.BlockSpec((rows, STEP), lambda step: (0, step))

    return pl.pallas_call(
        kernel,
        grid=(out_shapes[0].shape[1] // STEP,),
        out_shape=out_shapes,
        in_specs=[pl.BlockSpec(select.shape, lambda step: (0, 0, 0))] + [part(value.shape[0]) for value in values],
        out_specs=tuple(part(shape.shape[0]) for shape in out_shapes),
        compiler_params=PARAMS,
    )(select, *values)


def expert_kernel(y_ref, direct_ref, matrix_ref, weight_ref, cotangent_ref, *refs):
    arrived, refs = refs[:N_Y], refs[N_Y:]
    rows_ref, hidden_ref, grad_ref, direct_back_ref = refs[:4]
    back_refs = refs[4:]
    units = hidden_ref.shape[1]
    width = direct_ref.shape[1]
    count = arrived[0].shape[0]
    parts = [
        pl.ds(pl.multiple_of(((y_ref[0] + N_Y - k) & (N_Y - 1)) * count, count), count) for k in range(N_Y)
    ]
    for part, ref in zip(parts, arrived):
        rows_ref[part, :] = ref[...]
    pre = dot(direct_ref[...], matrix_ref[:width, :]) + dot(rows_ref[...], matrix_ref[width:, :])
    gate_pre, up_pre = pre[:, :units], pre[:, units:]
    weight = weight_ref[...]
    sigmoid_gate = jax.nn.sigmoid(gate_pre)
    activation = gate_pre * sigmoid_gate
    hidden_ref[...] = (activation * up_pre * weight).astype(jnp.bfloat16)
    act_slope = sigmoid_gate * (1.0 + gate_pre * (1.0 - sigmoid_gate))
    scaled = cotangent_ref[...].astype(jnp.float32) * weight
    grad_ref[:, :units] = (scaled * up_pre * act_slope).astype(jnp.bfloat16)
    grad_ref[:, units:] = (scaled * activation).astype(jnp.bfloat16)
    direct_back_ref[...] = dot(grad_ref[...], matrix_ref[:width, :], (1, 1)).astype(jnp.bfloat16)
    for part, ref in zip(parts, back_refs):
        ref[...] = dot(grad_ref[part, :], matrix_ref[width:, :], (1, 1)).astype(jnp.bfloat16)


def call(kernel, out_shape, *operands, scalars=0):
    return pl.pallas_call(
        kernel,
        out_shape=out_shape,
        in_specs=[pl.BlockSpec(memory_space=pltpu.SMEM)] * scalars + [WHOLE] * (len(operands) - scalars),
        out_specs=jax.tree.map(lambda _: WHOLE, out_shape),
        compiler_params=PARAMS,
    )(*operands)


def after(value, *others):
    return lax.optimization_barrier((value,) + others)[0]


def shards(tokens, expert_ids, route_weights, gate_weight, up_weight, cotangent):
    experts = N_Y * N_Z
    groups = lax.axis_size("dp")
    slot_count, units = cotangent.shape[2:]
    capacity = slot_count // experts
    row_slots = N_Z * capacity
    block, model_width = tokens.shape[1:]
    width = model_width - DIRECT

    def exchange(parts, sign):
        moved = [
            lax.ppermute(parts[k], "y", [(i, (i + sign * k) % N_Y) for i in range(N_Y)]) for k in range(1, N_Y)
        ]
        return [parts[0]] + moved

    def exchange_direct(rows):
        parts = rows.reshape(experts, 8, capacity * DIRECT // 8)
        return lax.all_to_all(parts, ("y", "z"), 0, 0, tiled=True).reshape(rows.shape)

    gathered = lax.all_gather(tokens[0, :, DIRECT:], "z", axis=0, tiled=True)

    told = call(routing_kernel, array((experts * 8, block)), expert_ids[0].T, route_weights[0].T)
    told = told.reshape(experts, 8, block)
    heard = lax.all_to_all(told, ("y", "z"), 0, 0, tiled=True)
    own_row = lax.dynamic_slice_in_dim(heard, lax.axis_index("y") * N_Z, N_Z, axis=0)
    rank = jnp.transpose(own_row[:, :N_Y], (1, 0, 2)).astype(jnp.int32)
    base = capacity * jnp.arange(N_Z, dtype=jnp.int32)[None, :, None]
    slot_of = jnp.where(rank >= 0, rank + base, -1).reshape(N_Y, N_Z * block)
    slot_of = lax.dynamic_slice_in_dim(jnp.concatenate((slot_of, slot_of)), lax.axis_index("y"), N_Y, axis=0)
    half_rows, half_tokens = N_Y * row_slots // HALVES, N_Z * block // HALVES
    pick_select, add_select = call(
        select_kernel,
        (array((HALVES, half_rows, half_tokens)), array((HALVES, half_tokens, half_rows))),
        slot_of,
        slot_of.T,
    )
    places = jnp.arange(capacity, dtype=jnp.int32).astype(jnp.bfloat16)
    weight_col = jnp.sum(
        jnp.where(
            heard[:, N_Y, None, :] == places[None, :, None],
            heard[:, N_Y + 1, None, :].astype(jnp.float32),
            0.0,
        ),
        axis=2,
    ).reshape(slot_count, 1) / 8.0
    slots = np.arange(slot_count, dtype=np.int32)[:, None]
    direct, direct_select = call(
        direct_pick_kernel,
        (array((slot_count, DIRECT)), array((slot_count, block))),
        told[:, N_Y],
        jnp.asarray(slots // capacity),
        jnp.asarray(slots % capacity),
        tokens[0, :, :DIRECT],
    )
    stacked = jnp.concatenate((gate_weight[0], up_weight[0]), axis=1)
    matrix = lax.all_to_all(
        jnp.broadcast_to(stacked[None], (groups,) + stacked.shape), "dp", 0, 0, tiled=True
    ).reshape(model_width, 2 * units)

    gathered, direct = lax.optimization_barrier(
        (gathered, direct.reshape(experts, 8, capacity * DIRECT // 8), weight_col, pick_select, add_select, matrix)
    )[:2]
    direct = exchange_direct(direct.reshape(slot_count, DIRECT))
    part = array((row_slots, width))
    picked = by_columns(pick_kernel, (part,) * N_Y, pick_select, gathered)
    results = call(
        expert_kernel,
        (
            array((slot_count, width)),
            array((slot_count, units)),
            array((slot_count, 2 * units)),
            array((slot_count, DIRECT)),
        )
        + (part,) * N_Y,
        lax.axis_index("y").astype(jnp.int32).reshape(1),
        direct,
        matrix,
        weight_col,
        cotangent[0, 0],
        *exchange(picked, 1),
        scalars=1,
    )
    rows, hidden, grads, direct_back = results[:4]

    direct_back = exchange_direct(direct_back)
    direct_back, *returned = lax.optimization_barrier((direct_back, *exchange(results[4:], -1)))
    (sums,) = by_columns(add_kernel, (array((N_Z * block, width)),), add_select, *returned)
    token_grads = lax.psum_scatter(sums, "z", scatter_dimension=0, tiled=True).astype(jnp.float32)

    direct_grads = dot(direct_select, after(direct_back, sums), (0, 0))
    late_grads = after(grads, sums)
    terms = jnp.concatenate(
        (
            dot(direct, late_grads, (0, 0)).astype(jnp.bfloat16),
            dot(rows, late_grads, (0, 0)).astype(jnp.bfloat16),
        ),
        axis=0,
    ).reshape(groups, model_width // groups, 2 * units)
    weight_grads = jnp.sum(lax.all_to_all(terms, "dp", 0, 0, tiled=True).astype(jnp.float32), axis=0)
    return (
        hidden[None, None],
        jnp.concatenate((direct_grads, token_grads), axis=1)[None],
        weight_grads[None, :, :units],
        weight_grads[None, :, units:],
    )


def solution(mesh):
    grid = Mesh(mesh.devices.reshape(mesh.shape["dp"], N_Y, N_Z), ("dp", "y", "z"))
    expert = ("y", "z")
    in_specs = (
        P("dp", expert, None),
        P("dp", expert, None),
        P("dp", expert, None),
        P(expert, "dp", None),
        P(expert, "dp", None),
        P("dp", expert, None, None),
    )
    out_specs = (
        P("dp", expert, None, None),
        P("dp", expert, None),
        P(expert, "dp", None),
        P(expert, "dp", None),
    )
    return jax.shard_map(shards, mesh=grid, in_specs=in_specs, out_specs=out_specs, check_vma=False)
```

```python
import functools

import jax
import jax.numpy as jnp
import numpy as np
from jax import lax
from jax.experimental import pallas as pl
from jax.experimental.pallas import tpu as pltpu
from jax.sharding import PartitionSpec as P

LINES = 8
QUARTERS = 4
LANES = 128
PARTS = 2
PARAMS = pltpu.CompilerParams(vmem_limit_bytes=48 * 1024 * 1024)
F32 = jnp.float32
BF16 = jnp.bfloat16


def call(kernel, out_shape, *operands):
    whole = pl.BlockSpec(memory_space=pltpu.VMEM)
    return pl.pallas_call(
        kernel,
        out_shape=out_shape,
        in_specs=[whole] * len(operands),
        out_specs=jax.tree.map(lambda _: whole, out_shape),
        compiler_params=PARAMS,
    )(*operands)


def array(shape, dtype=BF16):
    return jax.ShapeDtypeStruct(shape, dtype)


def hbm(shape):
    return pltpu.HBM(shape, BF16)


def iota(shape, dimension):
    return lax.broadcasted_iota(jnp.int32, shape, dimension)


def one_hot(condition):
    return jnp.where(condition, 1.0, 0.0).astype(BF16)


def dot(a, b, contract=(1, 0)):
    return lax.dot_general(a, b, (((contract[0],), (contract[1],)), ((), ())), preferred_element_type=F32)


def of_quarter(select, quarter):
    line = iota(select.shape, 0) & (LINES - 1)
    return jnp.where((line & (QUARTERS - 1)) == quarter, select, jnp.zeros_like(select))


def source_kernel(
    ids_in, weights_in, tokens_in, out_ref, main_ref, extra_ref, ids_ref, weights_ref, tokens_ref, fetched
):
    pairs = ((ids_in, ids_ref), (weights_in, weights_ref), (tokens_in, tokens_ref))
    copies = [pltpu.make_async_copy(here, there, fetched.at[i]) for i, (here, there) in enumerate(pairs)]
    for copy in copies:
        copy.start()
    for copy in copies[:2]:
        copy.wait()
    tokens, width = tokens_ref.shape
    step = width // QUARTERS
    shape = (out_ref.shape[0], tokens)
    row = iota(shape, 0)
    expert, line = row // LINES, row & (LINES - 1)
    hits = jnp.zeros(shape, F32)
    eighths = jnp.zeros(shape, F32)
    weights = weights_ref[...].astype(F32)
    for choice in range(ids_ref.shape[0]):
        named = ids_ref[choice : choice + 1, :] == expert
        hits = hits + jnp.where(named, 1.0, 0.0)
        eighths = eighths + jnp.where(named, weights[choice : choice + 1, :], 0.0)
    earlier = one_hot(iota((tokens, tokens), 0) < iota((tokens, tokens), 1))
    rank = jnp.where(hits > 0.0, dot(hits.astype(BF16), earlier), -1.0).astype(jnp.int32)
    is_main = rank == line
    is_extra = rank == LINES + line // QUARTERS
    main, extra = one_hot(is_main), one_hot(is_extra)
    main_ref[...] = main
    extra_ref[...] = extra
    copies[2].wait()
    out_ref[:, :width] = dot(main, tokens_ref[...]).astype(BF16)
    beside = dot(of_quarter(extra, 0), tokens_ref[:, :step])
    for quarter in range(1, QUARTERS):
        beside = beside + dot(of_quarter(extra, quarter), tokens_ref[:, quarter * step : (quarter + 1) * step])
    out_ref[:, width : width + step] = beside.astype(BF16)
    main_weight = jnp.sum(jnp.where(is_main, eighths, 0.0), axis=1, keepdims=True)
    extra_weight = jnp.sum(jnp.where(is_extra, eighths, 0.0), axis=1, keepdims=True)
    lane = iota((shape[0], LANES), 1)
    both = jnp.where(lane == 0, main_weight, jnp.where(lane == 1, extra_weight, 0.0))
    out_ref[:, width + step :] = both.astype(BF16)


def order_of(sources):
    slots = LINES + 2
    first = [source * slots + slot for source in range(sources) for slot in range(LINES)]
    return np.array(first + [source * slots + slot for slot in (8, 9) for source in range(sources)], np.int32)


def reorder_kernel(row_ref, values_ref, out_ref):
    move = one_hot(iota((row_ref.shape[0], values_ref.shape[0]), 1) == row_ref[...])
    out_ref[...] = dot(move, values_ref[...]).astype(BF16)


def lines_of(rows, lines, quarter):
    row = iota((rows, lines), 0)
    sources = rows // 2
    source, second = row & (sources - 1), row // sources
    return one_hot(iota((rows, lines), 1) == source * LINES + second * QUARTERS + quarter)


def expert_kernel(
    blocks_ref, matrix_ref, cotangent_ref, row_ref, hidden_ref, main_grad_ref, extra_grad_ref, extra_ref, back_ref
):
    lines, extras = blocks_ref.shape[0], extra_ref.shape[0]
    width = matrix_ref.shape[0]
    step = width // QUARTERS
    units = hidden_ref.shape[1]
    places = [lines_of(extras, lines, quarter) for quarter in range(QUARTERS)]
    beside = blocks_ref[:, width : width + step]
    for quarter in range(QUARTERS):
        extra_ref[:, quarter * step : (quarter + 1) * step] = dot(places[quarter], beside).astype(BF16)
    weights = blocks_ref[:, width + step :]
    main_weight = weights[:, 0:1].astype(F32)
    extra_weight = dot(places[0], weights)[:, 1:2]
    weight = jnp.concatenate((main_weight, extra_weight), axis=0) * 0.125

    pre = dot(jnp.concatenate((blocks_ref[:, :width], extra_ref[...]), axis=0), matrix_ref[...])
    gate_pre, up_pre = pre[:, :units], pre[:, units:]
    sigmoid_gate = jax.nn.sigmoid(gate_pre)
    activation = gate_pre * sigmoid_gate
    hidden = (activation * up_pre * weight).astype(BF16)
    act_slope = sigmoid_gate * (1.0 + gate_pre * (1.0 - sigmoid_gate))
    scaled = cotangent_ref[...].astype(F32) * weight
    grad_gate = (scaled * up_pre * act_slope).astype(BF16)
    grad_up = (scaled * activation).astype(BF16)
    grads = jnp.concatenate((grad_gate, grad_up), axis=1)
    main_grad_ref[...] = grads[:lines]
    extra_grad_ref[...] = grads[lines:]
    back = dot(grads, matrix_ref[...], (1, 1)).astype(BF16)
    back_ref[:, :width] = back[:lines]
    extra_back = back[lines:]
    beside = dot(places[0], extra_back[:, :step], (0, 0))
    for quarter in range(1, QUARTERS):
        beside = beside + dot(places[quarter], extra_back[:, quarter * step : (quarter + 1) * step], (0, 0))
    back_ref[:, width:] = beside.astype(BF16)
    move = one_hot(iota((row_ref.shape[0], hidden.shape[0]), 1) == row_ref[...])
    hidden_ref[...] = dot(move, hidden).astype(BF16)


def token_kernel(main_ref, extra_ref, blocks_ref, out_ref):
    width = out_ref.shape[1]
    step = width // QUARTERS
    extra = extra_ref[...]
    total = dot(main_ref[...], blocks_ref[:, :width], (0, 0))
    for quarter in range(QUARTERS):
        part = slice(quarter * step, (quarter + 1) * step)
        out_ref[:, part] = total[:, part] + dot(of_quarter(extra, quarter), blocks_ref[:, width:], (0, 0))


def shards(tokens, expert_ids, route_weights, gate_weight, up_weight, cotangent):
    experts = lax.axis_size("expert")
    slot_count, units = cotangent.shape[2:]
    block, width = tokens.shape[1:]
    lines, extras = experts * LINES, experts * 2
    step = width // QUARTERS

    def exchange(blocks):
        parts = blocks.reshape(experts, LINES, blocks.shape[1])
        return lax.all_to_all(parts, "expert", 0, 0, tiled=True).reshape(blocks.shape)

    sources = (expert_ids[0].T, route_weights[0].T, tokens[0])
    vmem = pl.BlockSpec(memory_space=pltpu.VMEM)
    out_blocks = ((lines, width + step + LANES), (lines, block), (lines, block))
    outgoing, main, extra = pl.pallas_call(
        source_kernel,
        grid=(1,),
        out_shape=(hbm((lines, width + step + LANES)), hbm((lines, block)), hbm((lines, block))),
        in_specs=[pl.BlockSpec(memory_space=pltpu.HBM)] * 3,
        out_specs=tuple(pl.BlockSpec(shape, lambda step: (0, 0)) for shape in out_blocks),
        scratch_shapes=[pltpu.VMEM(value.shape, value.dtype) for value in sources]
        + [pltpu.SemaphoreType.DMA((3,))],
        compiler_params=PARAMS,
    )(*[pltpu.with_memory_space_constraint(value, pltpu.HBM) for value in sources])
    arrived = exchange(outgoing)

    stacked = jnp.concatenate((gate_weight[0], up_weight[0]), axis=1)
    matrix = lax.all_gather(stacked, "dp", axis=0, tiled=True)
    part_slots, part_lines, part_extras = slot_count // PARTS, lines // PARTS, extras // PARTS
    order = order_of(experts // PARTS)
    rows_of = np.concatenate([order + part * part_slots for part in range(PARTS)])
    cotangent_rows = call(
        reorder_kernel, array((slot_count, units)), jnp.asarray(rows_of[:, None]), cotangent[0, 0]
    )

    def part_of(rows, columns):
        return pl.BlockSpec((rows, columns), lambda part: (part, 0))

    hidden, main_grads, extra_grads, extra_rows, back = pl.pallas_call(
        expert_kernel,
        grid=(PARTS,),
        out_shape=(
            array((slot_count, units)),
            hbm((lines, 2 * units)),
            hbm((extras, 2 * units)),
            hbm((extras, width)),
            hbm((lines, width + step)),
        ),
        in_specs=[
            part_of(part_lines, width + step + LANES),
            vmem,
            part_of(part_slots, units),
            vmem,
        ],
        out_specs=(
            part_of(part_slots, units),
            part_of(part_lines, 2 * units),
            part_of(part_extras, 2 * units),
            part_of(part_extras, width),
            part_of(part_lines, width + step),
        ),
        compiler_params=PARAMS,
    )(arrived, matrix, cotangent_rows, jnp.asarray(np.argsort(order).astype(np.int32)[:, None]))
    token_grads = call(token_kernel, array((block, width), F32), main, extra, exchange(back))

    terms = dot(arrived[:, :width], main_grads, (0, 0)) + dot(extra_rows, extra_grads, (0, 0))
    weight_grads = lax.psum_scatter(terms.astype(BF16), "dp", scatter_dimension=0, tiled=True).astype(F32)
    return (
        hidden[None, None],
        token_grads[None],
        weight_grads[None, :, :units],
        weight_grads[None, :, units:],
    )


def solution(mesh):
    in_specs = (
        P("dp", "expert", None),
        P("dp", "expert", None),
        P("dp", "expert", None),
        P("expert", "dp", None),
        P("expert", "dp", None),
        P("dp", "expert", None, None),
    )
    out_specs = (
        P("dp", "expert", None, None),
        P("dp", "expert", None),
        P("expert", "dp", None),
        P("expert", "dp", None),
    )
    return jax.shard_map(shards, mesh=mesh, in_specs=in_specs, out_specs=out_specs, check_vma=False)
```

```python
import functools

import jax
import jax.numpy as jnp
import numpy as np
from jax import lax
from jax.experimental import pallas as pl
from jax.experimental.pallas import tpu as pltpu
from jax.sharding import Mesh, PartitionSpec as P

LINES = 8
N_Y = 4
N_Z = 16
QUARTERS = 4
LANES = 128
PARTS = 2
PARAMS = pltpu.CompilerParams(vmem_limit_bytes=48 * 1024 * 1024)
F32 = jnp.float32
BF16 = jnp.bfloat16


def call(kernel, out_shape, *operands):
    whole = pl.BlockSpec(memory_space=pltpu.VMEM)
    return pl.pallas_call(
        kernel,
        out_shape=out_shape,
        in_specs=[whole] * len(operands),
        out_specs=jax.tree.map(lambda _: whole, out_shape),
        compiler_params=PARAMS,
    )(*operands)


def array(shape, dtype=BF16):
    return jax.ShapeDtypeStruct(shape, dtype)


def hbm(shape):
    return pltpu.HBM(shape, BF16)


def iota(shape, dimension):
    return lax.broadcasted_iota(jnp.int32, shape, dimension)


def one_hot(condition):
    return jnp.where(condition, 1.0, 0.0).astype(BF16)


def dot(a, b, contract=(1, 0)):
    return lax.dot_general(a, b, (((contract[0],), (contract[1],)), ((), ())), preferred_element_type=F32)


def of_quarter(select, quarter):
    line = iota(select.shape, 0) & (LINES - 1)
    return jnp.where((line & (QUARTERS - 1)) == quarter, select, jnp.zeros_like(select))


def source_kernel(
    ids_in, weights_in, tokens_in, out_ref, main_ref, extra_ref, table_ref, ids_ref, weights_ref, tokens_ref, fetched
):
    pairs = ((ids_in, ids_ref), (weights_in, weights_ref), (tokens_in, tokens_ref))
    copies = [pltpu.make_async_copy(here, there, fetched.at[i]) for i, (here, there) in enumerate(pairs)]
    for copy in copies:
        copy.start()
    for copy in copies[:2]:
        copy.wait()
    tokens, width = tokens_ref.shape
    step = width // QUARTERS
    shape = (out_ref.shape[0], tokens)
    row = iota(shape, 0)
    expert, line = row // LINES, row & (LINES - 1)
    hits = jnp.zeros(shape, F32)
    eighths = jnp.zeros(shape, F32)
    weights = weights_ref[...].astype(F32)
    for choice in range(ids_ref.shape[0]):
        named = ids_ref[choice : choice + 1, :] == expert
        hits = hits + jnp.where(named, 1.0, 0.0)
        eighths = eighths + jnp.where(named, weights[choice : choice + 1, :], 0.0)
    earlier = one_hot(iota((tokens, tokens), 0) < iota((tokens, tokens), 1))
    rank = jnp.where(hits > 0.0, dot(hits.astype(BF16), earlier), -1.0).astype(jnp.int32)
    is_main = rank == line
    is_extra = rank == LINES + line // QUARTERS
    main, extra = one_hot(is_main), one_hot(is_extra)
    main_ref[...] = jnp.where(is_main, eighths * 0.125, 0.0).astype(BF16)
    extra_ref[...] = jnp.where(is_extra, eighths * 0.125, 0.0).astype(BF16)
    copies[2].wait()
    out_ref[:, :width] = dot(main, tokens_ref[...]).astype(BF16)
    beside = dot(of_quarter(extra, 0), tokens_ref[:, :step])
    for quarter in range(1, QUARTERS):
        beside = beside + dot(of_quarter(extra, quarter), tokens_ref[:, quarter * step : (quarter + 1) * step])
    out_ref[:, width : width + step] = beside.astype(BF16)
    main_weight = jnp.sum(jnp.where(is_main, eighths, 0.0), axis=1, keepdims=True)
    extra_weight = jnp.sum(jnp.where(is_extra, eighths, 0.0), axis=1, keepdims=True)
    lane, line = iota((shape[0], LANES), 1), iota((shape[0], LANES), 0) & (LINES - 1)
    is_second = (lane == LINES + line // QUARTERS) & ((line & (QUARTERS - 1)) == 0)
    both = jnp.where(lane == line, main_weight, jnp.where(is_second, extra_weight, 0.0))
    experts = table_ref.shape[0]
    gather = one_hot(iota((experts, shape[0]), 1) // LINES == iota((experts, shape[0]), 0))
    table_ref[...] = dot(gather, both.astype(BF16)).astype(BF16)


def order_of(sources):
    slots = LINES + 2
    first = [source * slots + slot for source in range(sources) for slot in range(LINES)]
    return np.array(first + [source * slots + slot for slot in (8, 9) for source in range(sources)], np.int32)


def reorder_kernel(row_ref, values_ref, out_ref):
    move = one_hot(iota((row_ref.shape[0], values_ref.shape[0]), 1) == row_ref[...])
    out_ref[...] = dot(move, values_ref[...]).astype(BF16)


def lines_of(rows, lines, quarter):
    row = iota((rows, lines), 0)
    sources = rows // 2
    source, second = row & (sources - 1), row // sources
    return one_hot(iota((rows, lines), 1) == source * LINES + second * QUARTERS + quarter)


def rows_of_blocks(blocks_ref, places, width):
    step = width // QUARTERS
    beside = blocks_ref[:, width:]
    extra = jnp.concatenate([dot(place, beside).astype(BF16) for place in places], axis=1)
    return jnp.concatenate((blocks_ref[:, :width], extra), axis=0)


def places_of(lines):
    return [lines_of(lines // QUARTERS, lines, quarter) for quarter in range(QUARTERS)]


def back_kernel(blocks_ref, matrix_ref, cotangent_ref, back_ref):
    lines, width = blocks_ref.shape[0], matrix_ref.shape[0]
    step, units = width // QUARTERS, cotangent_ref.shape[1]
    places = places_of(lines)
    pre = dot(rows_of_blocks(blocks_ref, places, width), matrix_ref[...])
    gate_pre, up_pre = pre[:, :units], pre[:, units:]
    sigmoid_gate = jax.nn.sigmoid(gate_pre)
    act_slope = sigmoid_gate * (1.0 + gate_pre * (1.0 - sigmoid_gate))
    cotangent = cotangent_ref[...].astype(F32)
    grad_gate = (cotangent * up_pre * act_slope).astype(BF16)
    grad_up = (cotangent * (gate_pre * sigmoid_gate)).astype(BF16)
    back = dot(jnp.concatenate((grad_gate, grad_up), axis=1), matrix_ref[...], (1, 1)).astype(BF16)
    back_ref[:, :width] = back[:lines]
    beside = dot(places[0], back[lines:, :step], (0, 0))
    for quarter in range(1, QUARTERS):
        beside = beside + dot(places[quarter], back[lines:, quarter * step : (quarter + 1) * step], (0, 0))
    back_ref[:, width:] = beside.astype(BF16)


def hidden_kernel(
    blocks_ref, matrix_ref, cotangent_ref, weight_ref, row_ref, hidden_ref, main_grad_ref, extra_grad_ref, extra_ref
):
    lines, width = blocks_ref.shape[0], matrix_ref.shape[0]
    units = cotangent_ref.shape[1]
    rows = rows_of_blocks(blocks_ref, places_of(lines), width)
    extra_ref[...] = rows[lines:]
    pre = dot(rows, matrix_ref[...])
    weight = weight_ref[...] * 0.125
    gate_pre, up_pre = pre[:, :units], pre[:, units:]
    sigmoid_gate = jax.nn.sigmoid(gate_pre)
    activation = gate_pre * sigmoid_gate
    hidden = (activation * up_pre * weight).astype(BF16)
    act_slope = sigmoid_gate * (1.0 + gate_pre * (1.0 - sigmoid_gate))
    scaled = cotangent_ref[...].astype(F32) * weight
    grad_gate = (scaled * up_pre * act_slope).astype(BF16)
    grad_up = (scaled * activation).astype(BF16)
    grads = jnp.concatenate((grad_gate, grad_up), axis=1)
    main_grad_ref[...] = grads[:lines]
    extra_grad_ref[...] = grads[lines:]
    move = one_hot(iota((row_ref.shape[0], hidden.shape[0]), 1) == row_ref[...])
    hidden_ref[...] = dot(move, hidden).astype(BF16)


def token_kernel(main_ref, extra_ref, blocks_ref, out_ref):
    width = out_ref.shape[1]
    step = width // QUARTERS
    extra = extra_ref[...]
    total = dot(main_ref[...], blocks_ref[:, :width], (0, 0))
    for quarter in range(QUARTERS):
        part = slice(quarter * step, (quarter + 1) * step)
        out_ref[:, part] = total[:, part] + dot(of_quarter(extra, quarter), blocks_ref[:, width:], (0, 0))


def shards(tokens, expert_ids, route_weights, gate_weight, up_weight, cotangent):
    experts = N_Y * N_Z
    slot_count, units = cotangent.shape[2:]
    block, width = tokens.shape[1:]
    lines, extras = experts * LINES, experts * 2
    step = width // QUARTERS

    def exchange(blocks):
        parts = blocks.reshape(experts, LINES, blocks.shape[1])
        return lax.all_to_all(parts, ("y", "z"), 0, 0, tiled=True).reshape(blocks.shape)

    sources = (expert_ids[0].T, route_weights[0].T, tokens[0])
    vmem = pl.BlockSpec(memory_space=pltpu.VMEM)
    out_blocks = ((lines, width + step), (lines, block), (lines, block), (experts, LANES))
    outgoing, main, extra, table = pl.pallas_call(
        source_kernel,
        grid=(1,),
        out_shape=tuple(hbm(shape) for shape in out_blocks),
        in_specs=[pl.BlockSpec(memory_space=pltpu.HBM)] * 3,
        out_specs=tuple(pl.BlockSpec(shape, lambda step: (0, 0)) for shape in out_blocks),
        scratch_shapes=[pltpu.VMEM(value.shape, value.dtype) for value in sources]
        + [pltpu.SemaphoreType.DMA((3,))],
        compiler_params=PARAMS,
    )(*[pltpu.with_memory_space_constraint(value, pltpu.HBM) for value in sources])
    arrived = exchange(outgoing)

    stacked = jnp.concatenate((gate_weight[0], up_weight[0]), axis=1)
    matrix = lax.all_gather(stacked, "dp", axis=0, tiled=True)
    part_slots, part_lines, part_extras = slot_count // PARTS, lines // PARTS, extras // PARTS
    order = order_of(experts // PARTS)
    rows_of = np.concatenate([order + part * part_slots for part in range(PARTS)])
    cotangent_rows = call(
        reorder_kernel, array((slot_count, units)), jnp.asarray(rows_of[:, None]), cotangent[0, 0]
    )

    def part_of(rows, columns):
        return pl.BlockSpec((rows, columns), lambda part: (part, 0))

    tables = lax.all_gather(table, "z", axis=0).reshape(N_Z, N_Y, N_Z, LANES)
    tables = lax.dynamic_index_in_dim(tables, lax.axis_index("z"), 2, keepdims=False)
    tables = lax.all_gather(tables.reshape(N_Z * N_Y, LANES), "y", axis=0).reshape(experts, N_Y, LANES)
    tables = lax.dynamic_index_in_dim(tables, lax.axis_index("y"), 1, keepdims=False).astype(F32)
    first = tables[:, :LINES].reshape(PARTS, part_lines)
    second = tables[:, LINES : LINES + 2].reshape(PARTS, experts // PARTS, 2).transpose(0, 2, 1)
    weight_col = jnp.concatenate((first, second.reshape(PARTS, part_extras)), axis=1).reshape(slot_count, 1)
    arrived, weight_col = lax.optimization_barrier((arrived, weight_col))
    back = pl.pallas_call(
        back_kernel,
        grid=(PARTS,),
        out_shape=hbm((lines, width + step)),
        in_specs=[part_of(part_lines, width + step), vmem, part_of(part_slots, units)],
        out_specs=part_of(part_lines, width + step),
        compiler_params=PARAMS,
    )(arrived, matrix, cotangent_rows)

    arrived, _ = lax.optimization_barrier((arrived, back))
    hidden, main_grads, extra_grads, extra_rows = pl.pallas_call(
        hidden_kernel,
        grid=(PARTS,),
        out_shape=(
            array((slot_count, units)),
            hbm((lines, 2 * units)),
            hbm((extras, 2 * units)),
            hbm((extras, width)),
        ),
        in_specs=[
            part_of(part_lines, width + step),
            vmem,
            part_of(part_slots, units),
            part_of(part_slots, 1),
            vmem,
        ],
        out_specs=(
            part_of(part_slots, units),
            part_of(part_lines, 2 * units),
            part_of(part_extras, 2 * units),
            part_of(part_extras, width),
        ),
        compiler_params=PARAMS,
    )(arrived, matrix, cotangent_rows, weight_col, jnp.asarray(np.argsort(order).astype(np.int32)[:, None]))
    token_grads = call(token_kernel, array((block, width), F32), main, extra, exchange(back))

    terms = dot(arrived[:, :width], main_grads, (0, 0)) + dot(extra_rows, extra_grads, (0, 0))
    weight_grads = lax.psum_scatter(terms.astype(BF16), "dp", scatter_dimension=0, tiled=True).astype(F32)
    return (
        hidden[None, None],
        token_grads[None],
        weight_grads[None, :, :units],
        weight_grads[None, :, units:],
    )


def solution(mesh):
    grid = Mesh(mesh.devices.reshape(mesh.shape["dp"], N_Y, N_Z), ("dp", "y", "z"))
    expert = ("y", "z")
    in_specs = (
        P("dp", expert, None),
        P("dp", expert, None),
        P("dp", expert, None),
        P(expert, "dp", None),
        P(expert, "dp", None),
        P("dp", expert, None, None),
    )
    out_specs = (
        P("dp", expert, None, None),
        P("dp", expert, None),
        P(expert, "dp", None),
        P(expert, "dp", None),
    )
    return jax.shard_map(shards, mesh=grid, in_specs=in_specs, out_specs=out_specs, check_vma=False)
```

```python
import functools

import jax
import jax.numpy as jnp
import numpy as np
from jax import lax
from jax.experimental import pallas as pl
from jax.experimental.pallas import tpu as pltpu
from jax.sharding import PartitionSpec as P

LINES = 8
QUARTERS = 4
LANES = 128
PARTS = 2
PARAMS = pltpu.CompilerParams(vmem_limit_bytes=48 * 1024 * 1024)
F32 = jnp.float32
BF16 = jnp.bfloat16


def call(kernel, out_shape, *operands):
    whole = pl.BlockSpec(memory_space=pltpu.VMEM)
    return pl.pallas_call(
        kernel,
        out_shape=out_shape,
        in_specs=[whole] * len(operands),
        out_specs=jax.tree.map(lambda _: whole, out_shape),
        compiler_params=PARAMS,
    )(*operands)


def array(shape, dtype=BF16):
    return jax.ShapeDtypeStruct(shape, dtype)


def hbm(shape):
    return pltpu.HBM(shape, BF16)


def iota(shape, dimension):
    return lax.broadcasted_iota(jnp.int32, shape, dimension)


def one_hot(condition):
    return jnp.where(condition, 1.0, 0.0).astype(BF16)


def dot(a, b, contract=(1, 0)):
    return lax.dot_general(a, b, (((contract[0],), (contract[1],)), ((), ())), preferred_element_type=F32)


def of_quarter(select, quarter):
    line = iota(select.shape, 0) & (LINES - 1)
    return jnp.where((line & (QUARTERS - 1)) == quarter, select, jnp.zeros_like(select))


def source_kernel(
    ids_in, weights_in, tokens_in, out_ref, main_ref, extra_ref, ids_ref, weights_ref, tokens_ref, fetched
):
    pairs = ((ids_in, ids_ref), (weights_in, weights_ref), (tokens_in, tokens_ref))
    copies = [pltpu.make_async_copy(here, there, fetched.at[i]) for i, (here, there) in enumerate(pairs)]
    @pl.when(pl.program_id(0) == 0)
    def _():
        for copy in copies:
            copy.start()
        for copy in copies:
            copy.wait()

    tokens, width = tokens_ref.shape
    step = width // QUARTERS
    shape = (out_ref.shape[0], tokens)
    row = iota(shape, 0) + pl.program_id(0) * shape[0]
    expert, line = row // LINES, row & (LINES - 1)
    hits = jnp.zeros(shape, F32)
    eighths = jnp.zeros(shape, F32)
    weights = weights_ref[...].astype(F32)
    for choice in range(ids_ref.shape[0]):
        named = ids_ref[choice : choice + 1, :] == expert
        hits = hits + jnp.where(named, 1.0, 0.0)
        eighths = eighths + jnp.where(named, weights[choice : choice + 1, :], 0.0)
    earlier = one_hot(iota((tokens, tokens), 0) < iota((tokens, tokens), 1))
    rank = jnp.where(hits > 0.0, dot(hits.astype(BF16), earlier), -1.0).astype(jnp.int32)
    is_main = rank == line
    is_extra = rank == LINES + line // QUARTERS
    main, extra = one_hot(is_main), one_hot(is_extra)
    main_ref[...] = main
    extra_ref[...] = extra
    out_ref[:, :width] = dot(main, tokens_ref[...]).astype(BF16)
    beside = dot(of_quarter(extra, 0), tokens_ref[:, :step])
    for quarter in range(1, QUARTERS):
        beside = beside + dot(of_quarter(extra, quarter), tokens_ref[:, quarter * step : (quarter + 1) * step])
    out_ref[:, width : width + step] = beside.astype(BF16)
    main_weight = jnp.sum(jnp.where(is_main, eighths, 0.0), axis=1, keepdims=True)
    extra_weight = jnp.sum(jnp.where(is_extra, eighths, 0.0), axis=1, keepdims=True)
    lane = iota((shape[0], LANES), 1)
    both = jnp.where(lane == 0, main_weight, jnp.where(lane == 1, extra_weight, 0.0))
    out_ref[:, width + step :] = both.astype(BF16)


def order_of(sources):
    slots = LINES + 2
    first = [source * slots + slot for source in range(sources) for slot in range(LINES)]
    return np.array(first + [source * slots + slot for slot in (8, 9) for source in range(sources)], np.int32)


def reorder_kernel(row_ref, values_ref, out_ref):
    move = one_hot(iota((row_ref.shape[0], values_ref.shape[0]), 1) == row_ref[...])
    out_ref[...] = dot(move, values_ref[...]).astype(BF16)


def lines_of(rows, lines, quarter):
    row = iota((rows, lines), 0)
    sources = rows // 2
    source, second = row & (sources - 1), row // sources
    return one_hot(iota((rows, lines), 1) == source * LINES + second * QUARTERS + quarter)


def expert_kernel(
    blocks_ref, matrix_ref, cotangent_ref, row_ref, hidden_ref, main_grad_ref, extra_grad_ref, extra_ref, back_ref
):
    lines, extras = blocks_ref.shape[0], extra_ref.shape[0]
    width = matrix_ref.shape[0]
    step = width // QUARTERS
    units = hidden_ref.shape[1]
    places = [lines_of(extras, lines, quarter) for quarter in range(QUARTERS)]
    beside = blocks_ref[:, width : width + step]
    for quarter in range(QUARTERS):
        extra_ref[:, quarter * step : (quarter + 1) * step] = dot(places[quarter], beside).astype(BF16)
    weights = blocks_ref[:, width + step :]
    main_weight = weights[:, 0:1].astype(F32)
    extra_weight = dot(places[0], weights)[:, 1:2]
    weight = jnp.concatenate((main_weight, extra_weight), axis=0) * 0.125

    pre = dot(jnp.concatenate((blocks_ref[:, :width], extra_ref[...]), axis=0), matrix_ref[...])
    gate_pre, up_pre = pre[:, :units], pre[:, units:]
    sigmoid_gate = jax.nn.sigmoid(gate_pre)
    activation = gate_pre * sigmoid_gate
    hidden = (activation * up_pre * weight).astype(BF16)
    act_slope = sigmoid_gate * (1.0 + gate_pre * (1.0 - sigmoid_gate))
    scaled = cotangent_ref[...].astype(F32) * weight
    grad_gate = (scaled * up_pre * act_slope).astype(BF16)
    grad_up = (scaled * activation).astype(BF16)
    grads = jnp.concatenate((grad_gate, grad_up), axis=1)
    main_grad_ref[...] = grads[:lines]
    extra_grad_ref[...] = grads[lines:]
    back = dot(grads, matrix_ref[...], (1, 1)).astype(BF16)
    back_ref[:, :width] = back[:lines]
    extra_back = back[lines:]
    beside = dot(places[0], extra_back[:, :step], (0, 0))
    for quarter in range(1, QUARTERS):
        beside = beside + dot(places[quarter], extra_back[:, quarter * step : (quarter + 1) * step], (0, 0))
    back_ref[:, width:] = beside.astype(BF16)
    move = one_hot(iota((row_ref.shape[0], hidden.shape[0]), 1) == row_ref[...])
    hidden_ref[...] = dot(move, hidden).astype(BF16)


def token_kernel(main_ref, extra_ref, blocks_ref, beside_ref, out_ref):
    extra = extra_ref[...]
    line = iota(extra.shape, 0) & (QUARTERS - 1)
    own = jnp.where(line == pl.program_id(0), extra, jnp.zeros_like(extra))
    out_ref[...] = dot(main_ref[...], blocks_ref[...], (0, 0)) + dot(own, beside_ref[...], (0, 0))


def shards(tokens, expert_ids, route_weights, gate_weight, up_weight, cotangent):
    experts = lax.axis_size("expert")
    slot_count, units = cotangent.shape[2:]
    block, width = tokens.shape[1:]
    lines, extras = experts * LINES, experts * 2
    step = width // QUARTERS

    def exchange(blocks):
        parts = blocks.reshape(experts, LINES, blocks.shape[1])
        return lax.all_to_all(parts, "expert", 0, 0, tiled=True).reshape(blocks.shape)

    sources = (expert_ids[0].T, route_weights[0].T, tokens[0])
    vmem = pl.BlockSpec(memory_space=pltpu.VMEM)
    out_blocks = ((lines, width + step + LANES), (lines, block), (lines, block))
    outgoing, main, extra = pl.pallas_call(
        source_kernel,
        grid=(QUARTERS,),
        out_shape=(hbm((lines, width + step + LANES)), hbm((lines, block)), hbm((lines, block))),
        in_specs=[pl.BlockSpec(memory_space=pltpu.HBM)] * 3,
        out_specs=tuple(
            pl.BlockSpec((rows // QUARTERS, columns), lambda part: (part, 0)) for rows, columns in out_blocks
        ),
        scratch_shapes=[pltpu.VMEM(value.shape, value.dtype) for value in sources]
        + [pltpu.SemaphoreType.DMA((3,))],
        compiler_params=PARAMS,
    )(*[pltpu.with_memory_space_constraint(value, pltpu.HBM) for value in sources])
    arrived = exchange(outgoing)

    stacked = jnp.concatenate((gate_weight[0], up_weight[0]), axis=1)
    matrix = lax.all_gather(stacked, "dp", axis=0, tiled=True)
    part_slots, part_lines, part_extras = slot_count // PARTS, lines // PARTS, extras // PARTS
    order = order_of(experts // PARTS)
    rows_of = np.concatenate([order + part * part_slots for part in range(PARTS)])
    cotangent_rows = call(
        reorder_kernel, array((slot_count, units)), jnp.asarray(rows_of[:, None]), cotangent[0, 0]
    )

    def part_of(rows, columns):
        return pl.BlockSpec((rows, columns), lambda part: (part, 0))

    hidden, main_grads, extra_grads, extra_rows, back = pl.pallas_call(
        expert_kernel,
        grid=(PARTS,),
        out_shape=(
            array((slot_count, units)),
            hbm((lines, 2 * units)),
            hbm((extras, 2 * units)),
            hbm((extras, width)),
            hbm((lines, width + step)),
        ),
        in_specs=[
            part_of(part_lines, width + step + LANES),
            vmem,
            part_of(part_slots, units),
            vmem,
        ],
        out_specs=(
            part_of(part_slots, units),
            part_of(part_lines, 2 * units),
            part_of(part_extras, 2 * units),
            part_of(part_extras, width),
            part_of(part_lines, width + step),
        ),
        compiler_params=PARAMS,
    )(arrived, matrix, cotangent_rows, jnp.asarray(np.argsort(order).astype(np.int32)[:, None]))
    returned = exchange(back)
    token_grads = pl.pallas_call(
        token_kernel,
        grid=(QUARTERS,),
        out_shape=array((block, width), F32),
        in_specs=[
            pl.BlockSpec((lines, block), lambda part: (0, 0)),
            pl.BlockSpec((lines, block), lambda part: (0, 0)),
            pl.BlockSpec((lines, step), lambda part: (0, part)),
            pl.BlockSpec((lines, step), lambda part: (0, QUARTERS)),
        ],
        out_specs=pl.BlockSpec((block, step), lambda part: (0, part)),
        compiler_params=PARAMS,
    )(main, extra, returned, returned)

    terms = dot(arrived[:, :width], main_grads, (0, 0)) + dot(extra_rows, extra_grads, (0, 0))
    weight_grads = lax.psum_scatter(terms.astype(BF16), "dp", scatter_dimension=0, tiled=True).astype(F32)
    return (
        hidden[None, None],
        token_grads[None],
        weight_grads[None, :, :units],
        weight_grads[None, :, units:],
    )


def solution(mesh):
    in_specs = (
        P("dp", "expert", None),
        P("dp", "expert", None),
        P("dp", "expert", None),
        P("expert", "dp", None),
        P("expert", "dp", None),
        P("dp", "expert", None, None),
    )
    out_specs = (
        P("dp", "expert", None, None),
        P("dp", "expert", None),
        P("expert", "dp", None),
        P("expert", "dp", None),
    )
    return jax.shard_map(shards, mesh=mesh, in_specs=in_specs, out_specs=out_specs, check_vma=False)
```
